128 devices in a mesh: dp: 8 (over x_lo, y), fsdp: 16 (over x_hi, z, core).
Axes of the slice: x: 4 (x_hi: 2, x_lo: 2; x = x_hi * 2 + x_lo), y: 4, z: 4, core: 2. Of those that a mesh axis runs over, the one named last changes fastest.
Arguments:
- grads: bfloat16 [3, 2, 5120, 13824], P(None, None, 'dp', 'fsdp'), may hold values from -6 to 6
- basis_in: float32 [3, 2, 8, 5120, 128], P(None, None, 'dp', 'fsdp'), may hold values from -0.5 to 0.5
- eig_in: float32 [3, 2, 8, 5120], P(None, None, 'dp', 'fsdp'), may hold values from 0.3 to 3
- basis_out: float32 [3, 2, 8, 13824, 288], P(None, None, 'dp', 'fsdp'), may hold values from -0.375 to 0.375
- eig_out: float32 [3, 2, 8, 13824], P(None, None, 'dp', 'fsdp'), may hold values from 0.3 to 3
- owner: int32 [3, 2], replicated, may hold values from 0 to 7
Outputs:
- preconditioned: bfloat16 [3, 2, 5120, 13824], P(None, None, 'dp', 'fsdp')
The draws below stay inside these ranges and needn't reach their ends.
All inputs are finite; a program needn't handle non-finite values.
Results may differ from the reference program's by a relative error of at most 0.001.
Values sent between devices are 32-bit elements; how exact they have to be, the bound alone decides.
No kernel may reach another device: no remote copies, remote signals or barrier semaphores. Data moves between devices by JAX's collectives and lax.ppermute only.
A program may use at most 128 MiB of HBM per device.

```python
import math
import jax
import jax.numpy as jnp
from jax import lax

D = 5120
FF = 13824
BI = 128
BO = 288
LAYERS = 3
N_DP = 8


def plant(entries, key, least, high):
    longest = entries.shape.index(max(entries.shape))
    spots = []
    for shift in (0, 1):
        where = [jax.random.randint(jax.random.fold_in(key, axis), (), 0, length) for axis, length in enumerate(entries.shape)]
        where[longest] = (where[longest] + shift) % entries.shape[longest]
        spots.append(tuple(where))
    return entries.at[spots[0]].set(least).at[spots[1]].set(high)


def shard_levels(key, shape, split, least, high):
    def one(position, blocks):
        heights = jax.random.uniform(jax.random.fold_in(jax.random.fold_in(key, 6), position), (blocks,), jnp.float32, least / len(split), high / len(split))
        return jnp.repeat(jnp.exp(heights), shape[position] // blocks).reshape((-1,) + (1,) * (len(shape) - position - 1))

    level = one(*split[0])
    for cut in split[1:]:
        level = level * one(*cut)
    return level


def centred(rng, dims, spread, limit, split=(), kind=jnp.bfloat16):
    array = jax.random.normal(rng, dims, jnp.float32) * spread
    if len(split) > 0:
        array = shard_levels(rng, dims, split, -0.22, 0.18) * array
    return jnp.clip(array, min=-limit, max=limit).astype(kind)


def setup_inputs(seed: int = 0) -> dict:
    arg_keys = jax.random.split(jax.random.key(seed), 7)
    grads = centred(arg_keys[0], (LAYERS, 2, D, FF), 1.0, 6.0, ((2, 8), (3, 16)))
    basis_in = centred(arg_keys[1], (LAYERS, 2, N_DP, D, BI), BI ** -0.5, 0.5, ((2, 8), (3, 16)), jnp.float32)
    eig_in = jnp.clip(jnp.exp(math.log(3.0) - 2.3025851 * jax.random.uniform(arg_keys[2], (LAYERS, 2, N_DP, D), jnp.float32) ** shard_levels(arg_keys[2], (LAYERS, 2, N_DP, D), ((2, 8), (3, 16)), -0.2, 0.2)), 0.3, 3.0)
    basis_out = centred(arg_keys[3], (LAYERS, 2, N_DP, FF, BO), BO ** -0.5, 0.375, ((2, 8), (3, 16)), jnp.float32)
    eig_out = jnp.clip(jnp.exp(math.log(3.0) - 2.3025851 * jax.random.uniform(arg_keys[4], (LAYERS, 2, N_DP, FF), jnp.float32) ** shard_levels(arg_keys[4], (LAYERS, 2, N_DP, FF), ((2, 8), (3, 16)), -0.2, 0.2)), 0.3, 3.0)
    owner = plant(jax.random.randint(arg_keys[5], (LAYERS, 2), 0, N_DP), jax.random.fold_in(arg_keys[5], 1), 0, N_DP - 1).astype(jnp.int32)
    return {"grads": grads, "basis_in": basis_in, "eig_in": eig_in, "basis_out": basis_out, "eig_out": eig_out, "owner": owner}


damping = 0.1


def precondition(gradient, in_basis, in_values, out_basis, out_values):
    in_blocks = gradient.shape[0] // BI
    out_blocks = gradient.shape[1] // BO
    blocked = gradient.astype(jnp.float32).reshape(in_blocks, BI, out_blocks, BO)
    left_basis = in_basis.reshape(in_blocks, BI, BI)
    right_basis = out_basis.reshape(out_blocks, BO, BO)
    left_values = in_values.reshape(in_blocks, BI)
    right_values = out_values.reshape(out_blocks, BO)
    high = lax.Precision.HIGHEST
    turned = jnp.einsum('iak,iaob->ikob', left_basis, blocked, precision=high)
    rotated = jnp.einsum('ikob,obl->ikol', turned, right_basis, precision=high)
    scaled = rotated / (left_values[:, :, None, None] * right_values[None, None, :, :] + damping)
    back_turn = jnp.einsum('ikol,obl->ikob', scaled, right_basis, precision=high)
    result = jnp.einsum('iak,ikob->iaob', left_basis, back_turn, precision=high)
    return result.reshape(gradient.shape).astype(jnp.bfloat16)


def reference(grads, basis_in, eig_in, basis_out, eig_out, owner):
    layer_results = []
    for layer_slot in range(LAYERS):
        matrices = []
        for weight_slot in range(2):
            root_row = owner[layer_slot, weight_slot]
            matrices.append(precondition(grads[layer_slot, weight_slot],
                                         basis_in[layer_slot, weight_slot][root_row],
                                         eig_in[layer_slot, weight_slot][root_row],
                                         basis_out[layer_slot, weight_slot][root_row],
                                         eig_out[layer_slot, weight_slot][root_row]))
        layer_results.append(jnp.stack(matrices))
    return jnp.stack(layer_results)
```

```python
import jax
import jax.numpy as jnp
from jax import lax
from jax.experimental import pallas as pl
from jax.experimental.pallas import tpu as pltpu
from jax.sharding import PartitionSpec as P

BI = 128
BO = 288
M = 6
damping = 0.1
F32 = jnp.float32
BF16 = jnp.bfloat16

REM = 288
EIG = 336
ROWS = 344
IN_ROWS = 328
LANES_O = (0, 640, 1280)
LANES_R = (384, 1024)

BITS = (lambda v: v >> 2, lambda v: (v ^ (v >> 1)) & 1, lambda v: (v & 3) >> 1)
SWAPS = (lambda v: v ^ 4, lambda v: v ^ 1, lambda v: (v & 4) | (3 - (v & 3)))


def split(x):
    high = x.astype(BF16)
    return high, (x - high.astype(F32)).astype(BF16)


def pack_kernel(bits_ref, basis_ref, eig_ref, *refs):
    keeps, sends, wide = refs[:3], refs[3:6], refs[6]
    lane = lax.broadcasted_iota(jnp.int32, (48, 128), 1)
    wide[...] = jnp.zeros_like(wide)
    for o in range(3):
        first = bits_ref[o] == 0
        rows = slice(BO * o, BO * (o + 1))
        low, high = basis_ref[0, rows, 0:128], basis_ref[0, rows, 128:256]
        wide[:, 0:32] = basis_ref[0, rows, 256:288]
        rest = []
        for h in range(2):
            total = jnp.zeros((48, 128), F32)
            for g in range(6):
                part = wide[48 * g : 48 * (g + 1), :]
                shift = (16 * g - 16 * h) % 128
                if shift:
                    part = pltpu.roll(part, shift, 1)
                total = jnp.where((lane >= 16 * g) & (lane < 16 * g + 16), part, total)
            rest.append(total)
        eigs = eig_ref[0, o, 0], eig_ref[0, o, 1]
        for ref, a, b in ((keeps[o], 0, 1), (sends[o], 1, 0)):
            main = (low, high)
            ref[0, 0:REM, :] = jnp.where(first, main[a], main[b])
            ref[0, REM:EIG, :] = jnp.where(first, rest[a], rest[b])
            ref[0, EIG:ROWS, :] = jnp.where(first, eigs[a], eigs[b])


def pack(bits, basis, eig_rows):
    half = jax.ShapeDtypeStruct((M, ROWS, 128), F32)
    spec = pl.BlockSpec((1, ROWS, 128), lambda m, bits: (m, 0, 0))
    return pl.pallas_call(
        pack_kernel,
        out_shape=[half] * 6,
        grid_spec=pltpu.PrefetchScalarGridSpec(
            num_scalar_prefetch=1,
            grid=(M,),
            in_specs=[
                pl.BlockSpec((1, 3 * BO, BO), lambda m, bits: (m, 0, 0)),
                pl.BlockSpec((1, 3, 2, 8, 128), lambda m, bits: (m, 0, 0, 0, 0)),
            ],
            out_specs=[spec] * 6,
            scratch_shapes=[pltpu.VMEM((BO, 128), F32)],
        ),
        cost_estimate=pl.CostEstimate(flops=0, bytes_accessed=14_000_000, transcendentals=0),
        name="pack",
    )(bits, basis, eig_rows)


def left_kernel(core_ref, *refs):
    mine, other = refs[:3], refs[3:6]
    first_ref, second_ref, a_ref, whole = refs[6:]
    m = pl.program_id(0)
    core0 = core_ref[0] == 0
    for g in range(3):

        @pl.when(m // 2 == g)
        def _():
            x, y = mine[g][0], other[g][0]
            halves = jnp.where(core0, x, y), jnp.where(core0, y, x)
            for c in range(2):
                whole[320 * c : 320 * (c + 1), :] = halves[c][0:320]
                turned = halves[c][320:328].T
                for k, size in ((0, 128), (1, 128), (2, 64)):
                    a_ref[0, 320 * c + 128 * k : 320 * c + 128 * k + size, :] = jnp.broadcast_to(
                        turned[0:size, k : k + 1], (size, 128)
                    )

    for i in range(5):
        basis = whole[BI * i : BI * (i + 1), :]
        for ref, value in ((first_ref, basis.T), (second_ref, basis)):
            high, low = split(value)
            ref[0, i, 0:128, 0:128] = high
            ref[0, i, 0:128, 128:256] = high
            ref[0, i, 128:256, 0:128] = low
            ref[0, i, 128:256, 128:256] = low


def prepare_left(core, mine, other):
    def pick(g):
        return pl.BlockSpec((1, IN_ROWS, 128), lambda m, core: (jnp.clip(m - 2 * g, 0, 1), 0, 0))

    stacked = jax.ShapeDtypeStruct((M, 5, 256, 256), BF16)
    stacked_spec = pl.BlockSpec((1, 5, 256, 256), lambda m, core: (m, 0, 0, 0))
    return pl.pallas_call(
        left_kernel,
        out_shape=[stacked, stacked, jax.ShapeDtypeStruct((M, 640, 128), F32)],
        grid_spec=pltpu.PrefetchScalarGridSpec(
            num_scalar_prefetch=1,
            grid=(M,),
            in_specs=[pick(g) for g in (0, 1, 2, 0, 1, 2)],
            out_specs=[stacked_spec, stacked_spec, pl.BlockSpec((1, 640, 128), lambda m, core: (m, 0, 0))],
            scratch_shapes=[pltpu.VMEM((640, 128), F32)],
        ),
        cost_estimate=pl.CostEstimate(flops=0, bytes_accessed=12_000_000, transcendentals=0),
        name="left",
    )(core, *mine, *other)


def dot(a, b):
    return jnp.dot(a, b, preferred_element_type=F32)


def dot_nt(a, b):
    return lax.dot_general(a, b, (((1,), (1,)), ((), ())), preferred_element_type=F32)


def half_chain(grad_ref, halves, first_ref, a_ref, mains, rest, right, turned, stacked):
    lane = lax.broadcasted_iota(jnp.int32, (48, 128), 1)
    lane_b = lax.broadcasted_iota(jnp.int32, (BO, 128), 1)

    @pl.when(pl.program_id(0) == 0)
    def _():
        for ref in (*mains, right):
            ref[...] = jnp.zeros_like(ref)

    eig_rest = jnp.zeros((1, 128), F32)
    eigs = []
    for o in range(3):
        rows = slice(BO * o, BO * (o + 1))
        high, low = split(halves[o][0, 0:REM, :])
        mains[o][32 * o : 32 * o + BO, 0:128] = high
        mains[o][32 * o : 32 * o + BO, 128:256] = low
        at = LANES_O[o]
        right[rows, at : at + 128] = high
        right[rows, at + 128 : at + 256] = high
        right[rows, at + 256 : at + 384] = low
        packed = halves[o][0, REM:EIG, :]
        parts = []
        for g in range(6):
            near = (16 * o - 16 * g) % 128
            part = pltpu.roll(packed, near, 1) if near else packed
            far = pltpu.roll(packed, (near + 64) % 128, 1) if (near + 64) % 128 else packed
            part = jnp.where((lane >= 16 * o) & (lane < 16 * o + 16), part, 0.0)
            parts.append(jnp.where((lane >= 64 + 16 * o) & (lane < 80 + 16 * o), far, part))
        rest_high, rest_low = split(jnp.concatenate(parts, axis=0))
        rest[rows, 0:128] = rest_high
        rest[rows, 128:256] = rest_low
        mixed = jnp.where(lane_b < 64, rest_high.astype(F32), rest_low.astype(F32)).astype(BF16)
        for start in LANES_R:
            right[rows, start : start + 128] = mixed
            right[rows, start + 128 : start + 256] = mixed
        eigs.append(halves[o][0, EIG : EIG + 1, :])
        eig_rest = eig_rest + halves[o][0, EIG + 1 : EIG + 2, :]
    eigs.append(eig_rest)

    for o in range(4):
        if o < 3:
            product = dot(grad_ref[0, :, 256 * o : min(256 * o + 384, 864)], mains[o][...])
        else:
            product = dot(grad_ref[0], rest[...])
        high, low = split(product[:, 0:128] + product[:, 128:256])
        for i in range(5):
            turned[i, 0:128, 128 * o : 128 * (o + 1)] = high[BI * i : BI * (i + 1)]
            turned[i, 128:256, 128 * o : 128 * (o + 1)] = low[BI * i : BI * (i + 1)]

    for i in range(5):
        rows = slice(BI * i, BI * (i + 1))
        product = dot(first_ref[0, i], turned[i])
        rotated = product[0:128] + product[128:256]
        a = a_ref[0, rows, :]
        for o in range(4):
            scaled = rotated[:, 128 * o : 128 * (o + 1)] / (a * eigs[o] + damping)
            high, low = split(scaled)
            if o < 3:
                at = LANES_O[o]
                stacked[rows, at : at + 128] = high
                stacked[rows, at + 128 : at + 256] = low
                stacked[rows, at + 256 : at + 384] = high
            else:
                for at in LANES_R:
                    stacked[rows, at : at + 128] = high
                    stacked[rows, at + 128 : at + 256] = low

    for columns, lanes in (
        (slice(0, 256), slice(0, 640)),
        (slice(256, 512), slice(0, 1024)),
        (slice(512, 768), slice(640, 1664)),
        (slice(768, 864), slice(1024, 1664)),
    ):
        yield columns, dot_nt(stacked[:, lanes], right[columns, lanes])


def mine_kernel(grad_ref, h0, h1, h2, first_ref, a_ref, out_ref, m0, m1, m2, rest, right, turned, stacked):
    scratch = (m0, m1, m2), rest, right, turned, stacked
    for columns, value in half_chain(grad_ref, (h0, h1, h2), first_ref, a_ref, *scratch):
        out_ref[0, :, columns] = value


def other_kernel(
    grad_ref, h0, h1, h2, first_ref, a_ref, second_ref, part_ref, out_ref, m0, m1, m2, rest, right, turned, stacked, back
):
    scratch = (m0, m1, m2), rest, right, turned, stacked
    for columns, value in half_chain(grad_ref, (h0, h1, h2), first_ref, a_ref, *scratch):
        high, low = split(value + part_ref[0, :, columns])
        for i in range(5):
            back[i, 0:128, columns] = high[BI * i : BI * (i + 1)]
            back[i, 128:256, columns] = low[BI * i : BI * (i + 1)]
    for i in range(5):
        product = dot(second_ref[0, i], back[i])
        out_ref[0, BI * i : BI * (i + 1), :] = (product[0:128] + product[128:256]).astype(BF16)


def block(*shape):
    return pl.BlockSpec((1, *shape), lambda m: (m,) + (0,) * len(shape))


CHAIN_SCRATCH = [
    pltpu.VMEM((384, 256), BF16),
    pltpu.VMEM((384, 256), BF16),
    pltpu.VMEM((352, 256), BF16),
    pltpu.VMEM((864, 256), BF16),
    pltpu.VMEM((864, 1664), BF16),
    pltpu.VMEM((5, 256, 512), BF16),
    pltpu.VMEM((640, 1664), BF16),
]
CHAIN_IN = [block(640, 864)] + [block(ROWS, 128)] * 3 + [block(5, 256, 256), block(640, 128)]
CHAIN_PARAMS = pltpu.CompilerParams(vmem_limit_bytes=44 * 2**20)


def chain_mine(grads, halves, first, a):
    return pl.pallas_call(
        mine_kernel,
        out_shape=jax.ShapeDtypeStruct((M, 640, 864), F32),
        grid=(M,),
        in_specs=CHAIN_IN,
        out_specs=block(640, 864),
        scratch_shapes=CHAIN_SCRATCH,
        compiler_params=CHAIN_PARAMS,
        cost_estimate=pl.CostEstimate(flops=16_000_000_000, bytes_accessed=30_000_000, transcendentals=0),
        name="mine",
    )(grads, *halves, first, a)


def chain_other(grads, halves, first, a, second, part):
    return pl.pallas_call(
        other_kernel,
        out_shape=jax.ShapeDtypeStruct((M, 640, 864), BF16),
        grid=(M,),
        in_specs=CHAIN_IN + [block(5, 256, 256), block(640, 864)],
        out_specs=block(640, 864),
        scratch_shapes=CHAIN_SCRATCH + [pltpu.VMEM((5, 256, 864), BF16)],
        compiler_params=CHAIN_PARAMS,
        cost_estimate=pl.CostEstimate(flops=20_000_000_000, bytes_accessed=40_000_000, transcendentals=0),
        name="other",
    )(grads, *halves, first, a, second, part)


def eig_out_rows(eig):
    eig = eig.reshape(M, 3, BO)
    main = eig[:, :, :256].reshape(M, 3, 2, 1, 128)
    tail = eig[:, :, 256:].reshape(M, 3, 2, 1, 16)
    rows = []
    for o in range(3):
        once = jnp.pad(tail[:, o], ((0, 0), (0, 0), (0, 0), (16 * o, 48 - 16 * o)))
        rows.append(jnp.concatenate([once, once], axis=-1))
    tail = jnp.stack(rows, axis=1)
    return jnp.concatenate([main, tail, jnp.zeros((M, 3, 2, 6, 128), F32)], axis=3)


def shards(grads, basis_in, eig_in, basis_out, eig_out, owner):
    row = lax.axis_index("dp")
    column = lax.axis_index("fsdp")
    owner = owner.reshape(M)

    def exchange(x, axis, d):
        if axis == "dp":
            pairs = [(v, SWAPS[d](v)) for v in range(8)]
        else:
            pairs = [(f, 2 * SWAPS[d](f >> 1) + (f & 1)) for f in range(16)]
        return lax.ppermute(x, axis, pairs)

    def same_side(d, place, which=slice(None)):
        return (BITS[d](owner[which]) == BITS[d](place))[:, None, None]

    eig_rows = jnp.pad(eig_in.reshape(M, 320), ((0, 0), (0, 704))).reshape(M, 8, 128)
    in_copy = jnp.concatenate([basis_in.reshape(M, 320, 128), eig_rows], axis=1)
    flip = [(d * 16 + q * 2 + c, q * 16 + d * 2 + c) for d in range(8) for q in range(8) for c in range(2)]
    in_copy = lax.ppermute(in_copy, ("dp", "fsdp"), flip)

    bits = jnp.stack([BITS[d](row) for d in range(3)]).astype(jnp.int32)
    packed = pack(bits, basis_out.reshape(M, 3 * BO, BO), eig_out_rows(eig_out))
    keep, send = packed[:3], packed[3:]
    out = [exchange(send[o], "dp", o) for o in range(3)]
    out = [jnp.where(same_side(o, row), keep[o], out[o]) for o in range(3)]
    place = column >> 1
    inner = [in_copy[2 * g : 2 * g + 2] for g in range(3)]
    for step in range(3):
        for g in range(3):
            d = (g + step) % 3
            there = exchange(inner[g], "fsdp", d)
            inner[g] = jnp.where(same_side(d, place, slice(2 * g, 2 * g + 2)), inner[g], there)
        if step < 2:
            for o in range(3):
                d = (o + step + 1) % 3
                there = exchange(out[o], "dp", d)
                out[o] = jnp.where(same_side(d, row), out[o], there)
    across = [lax.ppermute(x, "fsdp", [(f, f ^ 1) for f in range(16)]) for x in inner]
    rest = [exchange(out[o], "dp", o) for o in range(3)]
    first, second, a = prepare_left((column & 1).reshape(1).astype(jnp.int32), inner, across)
    flat = grads.reshape(M, 640, 864)
    part = chain_mine(flat, out, first, a)
    result = chain_other(flat, rest, first, a, second, part)
    return result.reshape(grads.shape)


def solution(mesh):
    placed = (
        P(None, None, "dp", "fsdp"),
        P(None, None, "dp", "fsdp", None),
        P(None, None, "dp", "fsdp"),
        P(None, None, "dp", "fsdp", None),
        P(None, None, "dp", "fsdp"),
        P(),
    )
    return jax.shard_map(
        shards, mesh=mesh, in_specs=placed, out_specs=P(None, None, "dp", "fsdp"), check_vma=False
    )
```

```python
import jax
import jax.numpy as jnp
from jax import lax
from jax.experimental import pallas as pl
from jax.experimental.pallas import tpu as pltpu
from jax.sharding import PartitionSpec as P

BI = 128
BO = 288
M = 6
damping = 0.1
F32 = jnp.float32
BF16 = jnp.bfloat16

PIECE = 48
WIDE = 896
HALF = 3 * PIECE
IN_ROWS = 336

BITS = (lambda v: v >> 2, lambda v: (v ^ (v >> 1)) & 1, lambda v: (v & 3) >> 1)
SWAPS = (lambda v: v ^ 4, lambda v: v ^ 1, lambda v: (v & 4) | (3 - (v & 3)))


def split(x):
    high = x.astype(BF16)
    return high, (x - high.astype(F32)).astype(BF16)


def dot(a, b):
    return jnp.dot(a, b, preferred_element_type=F32)


def dot_tn(a, b):
    return lax.dot_general(a, b, (((0,), (0,)), ((), ())), preferred_element_type=F32)


def block(*shape):
    return pl.BlockSpec((1, *shape), lambda m, *_: (m,) + (0,) * len(shape))


CHAINS = ((0, 0), (1, 0), (2, 0), (0, 1), (1, 1))
LIST = 7
FINAL = 2 * M
CHAIN = FINAL + 3 * 2 * LIST
OWN = 5 * CHAIN
SIDE = OWN + LIST
FITS = SIDE + 3
SMALL = (3, 4, 5)
WHOLE = (M, M, M)


def table_kernel(owner_ref, place_ref, out_ref):
    def clear(i, carry):
        out_ref[i] = 0
        return carry

    lax.fori_loop(0, FITS + 1, clear, 0)
    owners = [owner_ref[m] for m in range(M)]
    corner = [[BITS[d](v) for v in owners] for d in range(3)]
    for c, (turn, axis) in enumerate(CHAINS):
        at = place_ref[axis]
        seen = [jnp.int32(0)] * 4
        steps, ranks = [], []
        for m in range(M):
            away = [corner[(turn + e) % 3][m] ^ BITS[(turn + e) % 3](at) for e in range(3)]
            step = jnp.where(away[2] == 1, 3, jnp.where(away[1] == 1, 2, away[0]))
            rank = seen[0]
            for k in range(1, 4):
                rank = jnp.where(step == k, seen[k], rank)
            for k in range(4):
                seen[k] = seen[k] + (step == k).astype(jnp.int32)
            out_ref[c * CHAIN + m] = step
            out_ref[c * CHAIN + M + m] = rank
            steps.append(step)
            ranks.append(rank)
        for k in range(1, 4):
            spot = jnp.int32(0)
            base = c * CHAIN + FINAL + 2 * LIST * (k - 1)
            for m in range(M):
                inside = steps[m] < k
                slot = jnp.where(inside, spot, LIST - 1)
                out_ref[base + slot] = steps[m]
                out_ref[base + LIST + slot] = ranks[m]
                if c == 0 and k == 1:
                    out_ref[OWN + slot] = m
                spot = spot + inside.astype(jnp.int32)
    for d in range(3):
        out_ref[SIDE + d] = BITS[d](place_ref[0])
    most = [jnp.int32(0)] * 3
    for m in range(M):
        same = [[(corner[d][m] == corner[d][n]).astype(jnp.int32) for n in range(M)] for d in range(3)]
        node = sum(same[0][n] * same[1][n] * same[2][n] for n in range(M))
        most[0] = jnp.maximum(most[0], node)
        for d in range(3):
            e, f = (d + 1) % 3, (d + 2) % 3
            most[1] = jnp.maximum(most[1], sum(same[e][n] * same[f][n] for n in range(M)))
            most[2] = jnp.maximum(most[2], sum(same[d]))
    fits = (most[0] <= SMALL[0]) & (most[1] <= SMALL[1]) & (most[2] <= SMALL[2])
    out_ref[FITS] = fits.astype(jnp.int32)


def make_tables(owner, place):
    smem = pl.BlockSpec(memory_space=pltpu.SMEM)
    return pl.pallas_call(
        table_kernel,
        out_shape=jax.ShapeDtypeStruct((FITS + 1,), jnp.int32),
        in_specs=[smem, smem],
        out_specs=smem,
        name="tables",
    )(owner, place)


def pack_kernel(table_ref, *refs):
    for t in range(3):
        refs[6 + t][0, :, 0:864] = refs[t][0]
        refs[6 + t][0, :, 864:WIDE] = refs[3 + t][0]


def pack(table, basis, eig, slots, other):
    def rows(t, lanes):
        def place(j, table):
            side = table[SIDE + t]
            return table[OWN + j], 2 * t + (1 - side if other else side), 0

        return pl.BlockSpec((1, PIECE, lanes), place)

    return pl.pallas_call(
        pack_kernel,
        out_shape=[jax.ShapeDtypeStruct((slots, PIECE, WIDE), F32)] * 3,
        grid_spec=pltpu.PrefetchScalarGridSpec(
            num_scalar_prefetch=1,
            grid=(slots,),
            in_specs=[rows(t, 864) for t in range(3)] + [rows(t, 32) for t in range(3)],
            out_specs=[block(PIECE, WIDE)] * 3,
        ),
        cost_estimate=pl.CostEstimate(flops=0, bytes_accessed=1_000_000 * slots, transcendentals=0),
        name="pack",
    )(table, basis, basis, basis, eig, eig, eig)


ANY = pl.BlockSpec(memory_space=pl.ANY)
SMEM = pl.BlockSpec(memory_space=pltpu.SMEM)
VMEM = pl.BlockSpec(memory_space=pltpu.VMEM)


def gather_kernel(slots, table_ref, basis_ref, eig_ref, out_ref, sems):
    copies = []
    for j in range(slots):
        m = table_ref[OWN + j]
        copies.append(pltpu.make_async_copy(basis_ref.at[m], out_ref.at[j, pl.ds(0, 320)], sems.at[2 * j]))
        copies.append(pltpu.make_async_copy(eig_ref.at[m], out_ref.at[j, pl.ds(320, 16)], sems.at[2 * j + 1]))
    for copy in copies:
        copy.start()
    for copy in copies:
        copy.wait()


def gather_own(table, basis, eig, slots):
    return pl.pallas_call(
        lambda *refs: gather_kernel(slots, *refs),
        out_shape=jax.ShapeDtypeStruct((slots, IN_ROWS, 128), F32),
        in_specs=[SMEM, ANY, ANY],
        out_specs=VMEM,
        scratch_shapes=[pltpu.SemaphoreType.DMA((2 * slots,))],
        cost_estimate=pl.CostEstimate(flops=0, bytes_accessed=400_000 * slots, transcendentals=0),
        name="gather",
    )(table, basis, eig)


def route_kernel(chains, step, slots, cut, count, table_ref, *refs):
    sources, outs, sems = refs[: count * len(chains)], refs[count * len(chains) : -1], refs[-1]
    for i, c in enumerate(chains):
        for j in range(slots):
            base = c * CHAIN + (j if step > 3 else FINAL + 2 * LIST * (step - 1) + j)
            arrived, slot = table_ref[base], table_ref[base + (M if step > 3 else LIST)]
            for k in range(count):
                source = sources[count * i + k].at[slot]
                if k == 0 and cut:
                    source = source.at[pl.ds(cut * i, cut)]

                @pl.when(arrived == k)
                def _():
                    pltpu.make_async_copy(source, outs[i].at[j], sems.at[i * slots + j]).start()

    for i in range(len(chains)):
        for j in range(slots):
            pltpu.make_async_copy(outs[i].at[j], outs[i].at[j], sems.at[i * slots + j]).wait()


def route(table, chains, step, slots, sources, shape, cut=0):
    count = len(sources[0])
    flat = [x for chain in sources for x in chain]
    return pl.pallas_call(
        lambda *refs: route_kernel(chains, step, slots, cut, count, *refs),
        out_shape=[jax.ShapeDtypeStruct((slots, *shape), F32)] * len(chains),
        in_specs=[SMEM] + [ANY] * len(flat),
        out_specs=[VMEM] * len(chains),
        scratch_shapes=[pltpu.SemaphoreType.DMA((len(chains) * slots,))],
        cost_estimate=pl.CostEstimate(flops=0, bytes_accessed=400_000 * slots, transcendentals=0),
        name="route",
    )(table, *flat)


def left_kernel(core_ref, *refs):
    mine, other = refs[:2], refs[2:4]
    first_ref, second_ref, a_ref, whole = refs[4:]
    core0 = core_ref[0] == 0
    for g, size in ((0, 168), (1, 152)):
        x, y = mine[g][0], other[g][0]
        low, high = jnp.where(core0, x, y), jnp.where(core0, y, x)
        whole[168 * g : 168 * g + size, :] = low[0:size]
        whole[320 + 168 * g : 320 + 168 * g + size, :] = high[0:size]
    a_ref[0, 0:2, :] = low[152:154]
    a_ref[0, 2:3, :] = low[154:155] + high[152:153]
    a_ref[0, 3:5, :] = high[153:155]
    a_ref[0, 5:8, :] = jnp.zeros((3, 128), F32)

    for i in range(5):
        basis = whole[BI * i : BI * (i + 1), :]
        for ref, value in ((first_ref, basis), (second_ref, basis.T)):
            high, low = split(value)
            for k in range(2):
                ref[0, i, 128 * k : 128 * (k + 1), 0:128] = high
                ref[0, i, 128 * k : 128 * (k + 1), 128:256] = low


def prepare_left(core, mine, other):
    stacked = jax.ShapeDtypeStruct((M, 5, 256, 256), BF16)
    return pl.pallas_call(
        left_kernel,
        out_shape=[stacked, stacked, jax.ShapeDtypeStruct((M, 8, 128), F32)],
        grid_spec=pltpu.PrefetchScalarGridSpec(
            num_scalar_prefetch=1,
            grid=(M,),
            in_specs=[block(IN_ROWS // 2, 128)] * 4,
            out_specs=[block(5, 256, 256), block(5, 256, 256), block(8, 128)],
            scratch_shapes=[pltpu.VMEM((640, 128), F32)],
        ),
        cost_estimate=pl.CostEstimate(flops=0, bytes_accessed=12_000_000, transcendentals=0),
        name="left",
    )(core, *mine, *other)


def half_chain(grad_ref, pieces, first_ref, a_ref, basis, turned, back, scaled):
    eigs = []
    for o in range(3):
        window = jnp.concatenate([ref[0, :, 256 * o : 256 * o + 384] for ref in pieces], axis=0)
        if o:
            window = pltpu.roll(window, 384 - 32 * o, 1)
        high, low = split(window[:, 0:BO])
        basis[o, 0:HALF, :] = high
        basis[o, HALF : 2 * HALF, :] = low
        back[o, 0:HALF, :] = high
        back[o, HALF : 2 * HALF, :] = high
        back[o, 2 * HALF : 3 * HALF, :] = low
        eigs.append(jnp.concatenate([ref[0, :, 768:WIDE][:, 96 + o : 97 + o] for ref in pieces], axis=0))

    for o in range(3):
        product = dot(basis[o], grad_ref[0, BO * o : BO * (o + 1), :])
        high, low = split(product[0:HALF] + product[HALF : 2 * HALF])
        for i in range(5):
            turned[i, HALF * o : HALF * (o + 1), 0:128] = high[:, BI * i : BI * (i + 1)]
            turned[i, HALF * o : HALF * (o + 1), 128:256] = low[:, BI * i : BI * (i + 1)]

    for i in range(5):
        product = dot(turned[i], first_ref[0, i])
        rotated = product[:, 0:128] + product[:, 128:256]
        columns = slice(BI * i, BI * (i + 1))
        for o in range(3):
            part = rotated[HALF * o : HALF * (o + 1)] / (eigs[o] * a_ref[0, i : i + 1, :] + damping)
            high, low = split(part)
            scaled[o, 0:HALF, columns] = high
            scaled[o, HALF : 2 * HALF, columns] = low
            scaled[o, 2 * HALF : 3 * HALF, columns] = high

    for o in range(3):
        yield o, dot_tn(back[o], scaled[o])


def mine_kernel(grad_ref, p0, p1, p2, first_ref, a_ref, out_ref, basis, turned, back, scaled):
    for o, value in half_chain(grad_ref, (p0, p1, p2), first_ref, a_ref, basis, turned, back, scaled):
        out_ref[0, BO * o : BO * (o + 1), :] = value


def other_kernel(
    grad_ref, p0, p1, p2, first_ref, a_ref, second_ref, part_ref, out_ref, basis, turned, back, scaled, whole
):
    for o, value in half_chain(grad_ref, (p0, p1, p2), first_ref, a_ref, basis, turned, back, scaled):
        rows = slice(BO * o, BO * (o + 1))
        high, low = split(value + part_ref[0, rows, :])
        for i in range(5):
            whole[i, rows, 0:128] = high[:, BI * i : BI * (i + 1)]
            whole[i, rows, 128:256] = low[:, BI * i : BI * (i + 1)]
    for i in range(5):
        product = dot(whole[i], second_ref[0, i])
        out_ref[0, :, BI * i : BI * (i + 1)] = (product[:, 0:128] + product[:, 128:256]).astype(BF16)


CHAIN_SCRATCH = [
    pltpu.VMEM((3, 2 * HALF, BO), BF16),
    pltpu.VMEM((5, 3 * HALF, 256), BF16),
    pltpu.VMEM((3, 3 * HALF, BO), BF16),
    pltpu.VMEM((3, 3 * HALF, 640), BF16),
]
CHAIN_IN = [block(864, 640)] + [block(PIECE, WIDE)] * 3 + [block(5, 256, 256), block(8, 128)]
CHAIN_PARAMS = pltpu.CompilerParams(vmem_limit_bytes=40 * 2**20)


def chain_mine(grads, pieces, first, a):
    return pl.pallas_call(
        mine_kernel,
        out_shape=jax.ShapeDtypeStruct((M, 864, 640), F32),
        grid=(M,),
        in_specs=CHAIN_IN,
        out_specs=block(864, 640),
        scratch_shapes=CHAIN_SCRATCH,
        compiler_params=CHAIN_PARAMS,
        cost_estimate=pl.CostEstimate(flops=16_000_000_000, bytes_accessed=30_000_000, transcendentals=0),
        name="mine",
    )(grads, *pieces, first, a)


def chain_other(grads, pieces, first, a, second, part):
    return pl.pallas_call(
        other_kernel,
        out_shape=jax.ShapeDtypeStruct((M, 864, 640), BF16),
        grid=(M,),
        in_specs=CHAIN_IN + [block(5, 256, 256), block(864, 640)],
        out_specs=block(864, 640),
        scratch_shapes=CHAIN_SCRATCH + [pltpu.VMEM((5, 864, 256), BF16)],
        compiler_params=CHAIN_PARAMS,
        cost_estimate=pl.CostEstimate(flops=20_000_000_000, bytes_accessed=40_000_000, transcendentals=0),
        name="other",
    )(grads, *pieces, first, a, second, part)


def exchange(x, axis, d):
    if axis == "dp":
        pairs = [(v, SWAPS[d](v)) for v in range(8)]
    else:
        pairs = [(f, 2 * SWAPS[d](f >> 1) + (f & 1)) for f in range(16)]
    return lax.ppermute(x, axis, pairs)


def together(arrays):
    return list(lax.optimization_barrier(tuple(arrays)))


def precondition(sizes, table, core, grads, basis_in, eig_in, basis, eig_out):
    flip = [(d * 16 + q * 2 + c, q * 16 + d * 2 + c) for d in range(8) for q in range(8) for c in range(2)]
    inner = gather_own(table, basis_in, eig_in, sizes[0])
    inner = lax.ppermute(inner, ("dp", "fsdp"), flip)

    out_chains, in_chains = (0, 1, 2), (3, 4)
    shape, cut = (PIECE, WIDE), IN_ROWS // 2
    held = [[x] for x in pack(table, basis, eig_out, sizes[0], False)]
    send = pack(table, basis, eig_out, sizes[0], True)
    in_held = [[inner], [inner]]
    in_send = [inner[:, cut * g : cut * (g + 1)] for g in range(2)]
    for step in range(1, 4):
        there = together([exchange(send[t], "dp", (t + step - 1) % 3) for t in range(3)])
        for t in range(3):
            held[t].append(there[t])
        in_there = together([exchange(in_send[g], "fsdp", (g + step - 1) % 3) for g in range(2)])
        for g in range(2):
            in_held[g].append(in_there[g])
        slots = sizes[step] if step < 3 else M
        send = route(table, out_chains, step + 1, slots, held, shape)
        in_send = route(table, in_chains, step + 1, slots, in_held, (cut, 128), cut)
    across = [lax.ppermute(x, "fsdp", [(f, f ^ 1) for f in range(16)]) for x in in_send]
    rest = [exchange(send[t], "dp", t) for t in range(3)]
    first, second, a = prepare_left(core, in_send, across)
    part = chain_mine(grads, send, first, a)
    return chain_other(grads, rest, first, a, second, part)


def shards(grads, basis_in, eig_in, basis_out, eig_out, owner):
    row = lax.axis_index("dp")
    column = lax.axis_index("fsdp")
    place, core = column >> 1, column & 1
    table = make_tables(owner.reshape(M), jnp.stack([row, place]).astype(jnp.int32))
    eig_rows = eig_in.reshape(M, 320)
    eig_rows = jnp.where(core == 0, jnp.pad(eig_rows, ((0, 0), (0, 64))), jnp.pad(eig_rows, ((0, 0), (64, 0))))
    eig_rows = jnp.pad(eig_rows.reshape(M, 3, 128), ((0, 0), (0, 13), (0, 0)))
    eig_cols = jnp.pad(jnp.swapaxes(eig_out.reshape(M, 3, BO), 1, 2), ((0, 0), (0, 0), (0, 29)))
    arrays = (
        table,
        core.reshape(1).astype(jnp.int32),
        jnp.swapaxes(grads.reshape(M, 640, 864), 1, 2),
        basis_in.reshape(M, 320, 128),
        eig_rows,
        jnp.swapaxes(basis_out.reshape(M, 864, BO), 1, 2),
        eig_cols,
    )
    result = lax.cond(
        table[FITS] == 1,
        lambda *args: precondition(SMALL, *args),
        lambda *args: precondition(WHOLE, *args),
        *arrays,
    )
    return jnp.swapaxes(result, 1, 2).reshape(grads.shape)


def solution(mesh):
    placed = (
        P(None, None, "dp", "fsdp"),
        P(None, None, "dp", "fsdp", None),
        P(None, None, "dp", "fsdp"),
        P(None, None, "dp", "fsdp", None),
        P(None, None, "dp", "fsdp"),
        P(),
    )
    return jax.shard_map(
        shards, mesh=mesh, in_specs=placed, out_specs=P(None, None, "dp", "fsdp"), check_vma=False
    )
```

```python
import functools

import jax
import jax.numpy as jnp
from jax import lax
from jax.experimental import pallas as pl
from jax.experimental.pallas import tpu as pltpu
from jax.sharding import PartitionSpec as P

BI = 128
BO = 288
M = 6
damping = 0.1
PARAMS = pltpu.CompilerParams(vmem_limit_bytes=62 * 2**20)
F32 = jnp.float32
BF16 = jnp.bfloat16

PIECE = 48
WIDE = 896
HALF = 3 * PIECE
IN_ROWS = 336

BITS = (lambda v: v >> 2, lambda v: (v ^ (v >> 1)) & 1, lambda v: (v & 3) >> 1)
SWAPS = (lambda v: v ^ 4, lambda v: v ^ 1, lambda v: (v & 4) | (3 - (v & 3)))


def split(x):
    high = x.astype(BF16)
    return high, (x - high.astype(F32)).astype(BF16)


def dot(a, b):
    return jnp.dot(a, b, preferred_element_type=F32)


def dot_tn(a, b):
    return lax.dot_general(a, b, (((0,), (0,)), ((), ())), preferred_element_type=F32)


def block(*shape):
    return pl.BlockSpec((1, *shape), lambda m, *_: (m,) + (0,) * len(shape))


CHAINS = ((0, 0), (1, 0), (2, 0), (0, 1))
LIST = 7
THIRD = 2 * M
CHAIN = THIRD + 2 * LIST
OWN = len(CHAINS) * CHAIN
SIDE = OWN + LIST
TIER = SIDE + 3
SIZES = ((2, 5), (3, 5), (M, M))


def table_kernel(owner_ref, place_ref, out_ref):
    def clear(i, carry):
        out_ref[i] = 0
        return carry

    lax.fori_loop(0, TIER + 1, clear, 0)
    owners = [owner_ref[m] for m in range(M)]
    corner = [[BITS[d](v) for v in owners] for d in range(3)]
    row = [BITS[d](place_ref[0]) for d in range(3)]
    column = [BITS[d](place_ref[1]) for d in range(3)]
    for c, (turn, axis) in enumerate(CHAINS):
        seen = [jnp.int32(0)] * 5
        spot = jnp.int32(0)
        for m in range(M):
            away = [corner[(turn + e) % 3][m] ^ row[(turn + e) % 3] for e in range(3)]
            if axis:
                away = [away[e] ^ column[(turn + e) % 3] for e in range(3)]
            array = jnp.where(away[2] == 1, 4, away[0] + 2 * away[1])
            slot = seen[0]
            for k in range(1, 5):
                slot = jnp.where(array == k, seen[k], slot)
            seen = [seen[k] + (array == k).astype(jnp.int32) for k in range(5)]
            out_ref[c * CHAIN + m] = array
            out_ref[c * CHAIN + M + m] = slot
            here = jnp.where(array < 4, spot, LIST - 1)
            out_ref[c * CHAIN + THIRD + here] = array
            out_ref[c * CHAIN + THIRD + LIST + here] = slot
            spot = spot + (array < 4).astype(jnp.int32)
            if c == 0:
                out_ref[OWN + jnp.where(array == 0, slot, LIST - 1)] = m
    for d in range(3):
        out_ref[SIDE + d] = row[d]
    node, face = jnp.int32(0), jnp.int32(0)
    for m in range(M):
        same = [[(corner[d][m] == corner[d][n]).astype(jnp.int32) for n in range(M)] for d in range(3)]
        node = jnp.maximum(node, sum(same[0][n] * same[1][n] * same[2][n] for n in range(M)))
        for d in range(3):
            face = jnp.maximum(face, sum(same[d]))
    tier = jnp.int32(len(SIZES) - 1)
    for k in range(len(SIZES) - 2, -1, -1):
        tier = jnp.where((node <= SIZES[k][0]) & (face <= SIZES[k][1]), k, tier)
    out_ref[TIER] = tier


def make_tables(owner, place):
    smem = pl.BlockSpec(memory_space=pltpu.SMEM)
    return pl.pallas_call(
        table_kernel,
        out_shape=jax.ShapeDtypeStruct((TIER + 1,), jnp.int32),
        in_specs=[smem, smem],
        out_specs=smem,
        name="tables",
    )(owner, place)


def pack_kernel(table_ref, *refs):
    for k in range(6):
        refs[12 + k][0, :, 0:864] = refs[k][0]
        refs[12 + k][0, :, 864:WIDE] = refs[6 + k][0]


def pack(table, basis, eig, slots):
    def rows(t, other, lanes):
        def place(j, table):
            side = table[SIDE + t]
            return table[OWN + j], 2 * t + (1 - side if other else side), 0

        return pl.BlockSpec((1, PIECE, lanes), place)

    halves = [(t, other) for other in (True, False) for t in range(3)]
    out = pl.pallas_call(
        pack_kernel,
        out_shape=[jax.ShapeDtypeStruct((slots, PIECE, WIDE), F32)] * 6,
        grid_spec=pltpu.PrefetchScalarGridSpec(
            num_scalar_prefetch=1,
            grid=(slots,),
            in_specs=[rows(*half, 864) for half in halves] + [rows(*half, 32) for half in halves],
            out_specs=[block(PIECE, WIDE)] * 6,
        ),
        cost_estimate=pl.CostEstimate(flops=0, bytes_accessed=2_000_000 * slots, transcendentals=0),
        name="pack",
    )(table, *[basis] * 6, *[eig] * 6)
    return out[:3], out[3:]


ANY = pl.BlockSpec(memory_space=pl.ANY)
SMEM = pl.BlockSpec(memory_space=pltpu.SMEM)
VMEM = pl.BlockSpec(memory_space=pltpu.VMEM)


def gather_kernel(slots, table_ref, basis_ref, eig_ref, out_ref, sems):
    copies = []
    for j in range(slots):
        m = table_ref[OWN + j]
        copies.append(pltpu.make_async_copy(basis_ref.at[m], out_ref.at[j, pl.ds(0, 320)], sems.at[2 * j]))
        copies.append(pltpu.make_async_copy(eig_ref.at[m], out_ref.at[j, pl.ds(320, 16)], sems.at[2 * j + 1]))
    for copy in copies:
        copy.start()
    for copy in copies:
        copy.wait()


def gather_own(table, basis, eig, slots):
    return pl.pallas_call(
        lambda *refs: gather_kernel(slots, *refs),
        out_shape=jax.ShapeDtypeStruct((slots, IN_ROWS, 128), F32),
        in_specs=[SMEM, ANY, ANY],
        out_specs=VMEM,
        scratch_shapes=[pltpu.SemaphoreType.DMA((2 * slots,))],
        cost_estimate=pl.CostEstimate(flops=0, bytes_accessed=400_000 * slots, transcendentals=0),
        name="gather",
    )(table, basis, eig)


def route_kernel(chains, slots, count, table_ref, *refs):
    sources, outs, sems = refs[: count * len(chains)], refs[count * len(chains) : -1], refs[-1]
    for i, c in enumerate(chains):
        for j in range(slots):
            base = c * CHAIN + (THIRD + j if count == 4 else j)
            array, slot = table_ref[base], table_ref[base + (LIST if count == 4 else M)]
            for k in range(count):

                @pl.when(array == k)
                def _():
                    pltpu.make_async_copy(sources[count * i + k].at[slot], outs[i].at[j], sems.at[i * slots + j]).start()

    for i in range(len(chains)):
        for j in range(slots):
            pltpu.make_async_copy(outs[i].at[j], outs[i].at[j], sems.at[i * slots + j]).wait()


def route(table, chains, slots, sources, shape):
    count = len(sources[0])
    flat = [x for chain in sources for x in chain]
    return pl.pallas_call(
        functools.partial(route_kernel, chains, slots, count),
        out_shape=[jax.ShapeDtypeStruct((slots, *shape), F32)] * len(chains),
        in_specs=[SMEM] + [ANY] * len(flat),
        out_specs=[VMEM] * len(chains),
        scratch_shapes=[pltpu.SemaphoreType.DMA((len(chains) * slots,))],
        cost_estimate=pl.CostEstimate(flops=0, bytes_accessed=400_000 * slots, transcendentals=0),
        name="route",
    )(table, *flat)


def join_left(core_ref, mine, other, whole, a_scratch):
    core0 = core_ref[0] == 0
    low = jnp.where(core0, mine[0], other[0])
    high = jnp.where(core0, other[0], mine[0])
    whole[0:320, :] = low[0:320]
    whole[320:640, :] = high[0:320]
    a_scratch[0:2, :] = low[320:322]
    a_scratch[2:3, :] = low[322:323] + high[320:321]
    a_scratch[3:5, :] = high[321:323]


def doubled(value):
    high, low = split(value)
    both = jnp.concatenate([high, low], axis=1)
    return jnp.concatenate([both, both], axis=0)


def half_chain(grad_ref, pieces, whole, a_scratch, basis, turned, back, scaled):
    eigs = []
    for o in range(3):
        window = jnp.concatenate([ref[0, :, 256 * o : 256 * o + 384] for ref in pieces], axis=0)
        if o:
            window = pltpu.roll(window, 384 - 32 * o, 1)
        high, low = split(window[:, 0:BO])
        basis[o, 0:HALF, :] = high
        basis[o, HALF : 2 * HALF, :] = low
        back[o, 0:HALF, :] = high
        back[o, HALF : 2 * HALF, :] = high
        back[o, 2 * HALF : 3 * HALF, :] = low
        eigs.append(jnp.concatenate([ref[0, :, 768:WIDE][:, 96 + o : 97 + o] for ref in pieces], axis=0))

    for o in range(3):
        product = dot(basis[o], grad_ref[0, BO * o : BO * (o + 1), :])
        high, low = split(product[0:HALF] + product[HALF : 2 * HALF])
        for i in range(5):
            turned[i, HALF * o : HALF * (o + 1), 0:128] = high[:, BI * i : BI * (i + 1)]
            turned[i, HALF * o : HALF * (o + 1), 128:256] = low[:, BI * i : BI * (i + 1)]

    for i in range(5):
        product = dot(turned[i], doubled(whole[BI * i : BI * (i + 1), :]))
        rotated = product[:, 0:128] + product[:, 128:256]
        columns = slice(BI * i, BI * (i + 1))
        for o in range(3):
            part = rotated[HALF * o : HALF * (o + 1)] / (eigs[o] * a_scratch[i : i + 1, :] + damping)
            high, low = split(part)
            scaled[o, 0:HALF, columns] = high
            scaled[o, HALF : 2 * HALF, columns] = low
            scaled[o, 2 * HALF : 3 * HALF, columns] = high

    for o in range(3):
        yield o, dot_tn(back[o], scaled[o])


def mine_kernel(core_ref, grad_ref, p0, p1, p2, left, across, out_ref, *scratch):
    join_left(core_ref, left, across, *scratch[:2])
    for o, value in half_chain(grad_ref, (p0, p1, p2), *scratch):
        out_ref[0, BO * o : BO * (o + 1), :] = value


def other_kernel(core_ref, grad_ref, p0, p1, p2, left, across, part_ref, out_ref, *scratch):
    *scratch, whole = scratch
    join_left(core_ref, left, across, *scratch[:2])
    for o, value in half_chain(grad_ref, (p0, p1, p2), *scratch):
        rows = slice(BO * o, BO * (o + 1))
        high, low = split(value + part_ref[0, rows, :])
        for i in range(5):
            whole[i, rows, 0:128] = high[:, BI * i : BI * (i + 1)]
            whole[i, rows, 128:256] = low[:, BI * i : BI * (i + 1)]
    for i in range(5):
        product = dot(whole[i], doubled(scratch[0][BI * i : BI * (i + 1), :].T))
        out_ref[0, :, BI * i : BI * (i + 1)] = (product[:, 0:128] + product[:, 128:256]).astype(BF16)


CHAIN_SCRATCH = [
    pltpu.VMEM((640, 128), F32),
    pltpu.VMEM((8, 128), F32),
    pltpu.VMEM((3, 2 * HALF, BO), BF16),
    pltpu.VMEM((5, 3 * HALF, 256), BF16),
    pltpu.VMEM((3, 3 * HALF, BO), BF16),
    pltpu.VMEM((3, 3 * HALF, 640), BF16),
]
CHAIN_IN = [block(864, 640)] + [block(PIECE, WIDE)] * 3 + [block(IN_ROWS, 128)] * 2


def chain_mine(core, grads, pieces, left):
    return pl.pallas_call(
        mine_kernel,
        out_shape=jax.ShapeDtypeStruct((M, 864, 640), F32),
        grid_spec=pltpu.PrefetchScalarGridSpec(
            num_scalar_prefetch=1,
            grid=(M,),
            in_specs=CHAIN_IN,
            out_specs=block(864, 640),
            scratch_shapes=CHAIN_SCRATCH,
        ),
        compiler_params=PARAMS,
        cost_estimate=pl.CostEstimate(flops=16_000_000_000, bytes_accessed=30_000_000, transcendentals=0),
        name="mine",
    )(core, grads, *pieces, *left)


def chain_other(core, grads, pieces, left, part):
    return pl.pallas_call(
        other_kernel,
        out_shape=jax.ShapeDtypeStruct((M, 864, 640), BF16),
        grid_spec=pltpu.PrefetchScalarGridSpec(
            num_scalar_prefetch=1,
            grid=(M,),
            in_specs=CHAIN_IN + [block(864, 640)],
            out_specs=block(864, 640),
            scratch_shapes=CHAIN_SCRATCH + [pltpu.VMEM((5, 864, 256), BF16)],
        ),
        compiler_params=PARAMS,
        cost_estimate=pl.CostEstimate(flops=20_000_000_000, bytes_accessed=40_000_000, transcendentals=0),
        name="other",
    )(core, grads, *pieces, *left, part)


def exchange(x, axis, d):
    if axis == "dp":
        pairs = [(v, SWAPS[d % 3](v)) for v in range(8)]
    else:
        pairs = [(f, 2 * SWAPS[d](f >> 1) + (f & 1)) for f in range(16)]
    return lax.ppermute(x, axis, pairs)


def apart(v, w):
    bits = [f(v) ^ f(w) for f in BITS]
    return next(u for u in range(8) if [f(u) for f in BITS] == bits)


def together(arrays):
    return list(lax.optimization_barrier(tuple(arrays)))


def precondition(sizes, table, core, grads, basis_in, eig_in, basis, eig_out):
    both = ("dp", "fsdp")
    every = [(d, q, c) for d in range(8) for q in range(8) for c in range(2)]
    inner = gather_own(table, basis_in, eig_in, sizes[0])
    inner = lax.ppermute(inner, both, [(d * 16 + q * 2 + c, d * 16 + 2 * apart(d, q) + c) for d, q, c in every])
    inner = lax.ppermute(inner, both, [(d * 16 + q * 2 + c, apart(d, q) * 16 + q * 2 + c) for d, q, c in every])

    shape, in_shape = (PIECE, WIDE), (IN_ROWS, 128)
    send, keep = pack(table, basis, eig_out, sizes[0])
    first = [exchange(send[t], "dp", t) for t in range(3)]
    second = [exchange(keep[t], "dp", t + 1) for t in range(3)]
    first = together(first)
    follow = [exchange(first[t], "dp", t + 1) for t in range(3)]
    in_first = exchange(inner, "fsdp", 0)
    in_second = exchange(inner, "fsdp", 1)
    in_follow = exchange(in_first, "fsdp", 1)
    arrived = together([*second, *follow])
    held = [[keep[t], first[t], arrived[t], arrived[3 + t]] for t in range(3)]
    send = route(table, (0, 1, 2), sizes[1], held, shape)
    third = [exchange(send[t], "dp", t + 2) for t in range(3)]
    in_second, in_follow = together([in_second, in_follow, *send])[:2]
    in_held = [inner, in_first, in_second, in_follow]
    in_third = exchange(route(table, (3,), sizes[1], [in_held], in_shape)[0], "fsdp", 2)
    third = together(third)
    send = route(table, (0, 1, 2), M, [[*held[t], third[t]] for t in range(3)], shape)
    rest = [exchange(send[t], "dp", t) for t in range(3)]
    in_third = together([in_third, *send])[0]
    left = route(table, (3,), M, [[*in_held, in_third]], in_shape)[0]
    left = [left, lax.ppermute(left, "fsdp", [(f, f ^ 1) for f in range(16)])]
    part = chain_mine(core, grads, send, left)
    return chain_other(core, grads, rest, left, part)


def shards(grads, basis_in, eig_in, basis_out, eig_out, owner):
    row = lax.axis_index("dp")
    column = lax.axis_index("fsdp")
    place, core = column >> 1, column & 1
    table = make_tables(owner.reshape(M), jnp.stack([row, place]).astype(jnp.int32))
    eig_rows = eig_in.reshape(M, 320)
    eig_rows = jnp.where(core == 0, jnp.pad(eig_rows, ((0, 0), (0, 64))), jnp.pad(eig_rows, ((0, 0), (64, 0))))
    eig_rows = jnp.pad(eig_rows.reshape(M, 3, 128), ((0, 0), (0, 13), (0, 0)))
    eig_cols = jnp.pad(jnp.swapaxes(eig_out.reshape(M, 3, BO), 1, 2), ((0, 0), (0, 0), (0, 29)))
    arrays = (
        table,
        core.reshape(1).astype(jnp.int32),
        jnp.swapaxes(grads.reshape(M, 640, 864), 1, 2),
        basis_in.reshape(M, 320, 128),
        eig_rows,
        jnp.swapaxes(basis_out.reshape(M, 864, BO), 1, 2),
        eig_cols,
    )
    plans = [functools.partial(precondition, sizes) for sizes in SIZES]
    result = lax.switch(table[TIER], plans, *arrays)
    return jnp.swapaxes(result, 1, 2).reshape(grads.shape)


def solution(mesh):
    placed = (
        P(None, None, "dp", "fsdp"),
        P(None, None, "dp", "fsdp", None),
        P(None, None, "dp", "fsdp"),
        P(None, None, "dp", "fsdp", None),
        P(None, None, "dp", "fsdp"),
        P(),
    )
    return jax.shard_map(
        shards, mesh=mesh, in_specs=placed, out_specs=P(None, None, "dp", "fsdp"), check_vma=False
    )
```

```python
import functools

import jax
import jax.numpy as jnp
from jax import lax
from jax.experimental import pallas as pl
from jax.experimental.pallas import tpu as pltpu
from jax.sharding import PartitionSpec as P

BI = 128
BO = 288
M = 6
damping = 0.1
PARAMS = pltpu.CompilerParams(vmem_limit_bytes=62 * 2**20)
F32 = jnp.float32
BF16 = jnp.bfloat16

PIECE = 48
WIDE = 896
HALF = 3 * PIECE
IN_ROWS = 336
PARTS = 3

BITS = (lambda v: v >> 2, lambda v: (v ^ (v >> 1)) & 1, lambda v: (v & 3) >> 1)
SWAPS = (lambda v: v ^ 4, lambda v: v ^ 1, lambda v: (v & 4) | (3 - (v & 3)))


def split(x):
    high = x.astype(BF16)
    return high, (x - high.astype(F32)).astype(BF16)


def dot(a, b):
    return jnp.dot(a, b, preferred_element_type=F32)


def dot_tn(a, b):
    return lax.dot_general(a, b, (((0,), (0,)), ((), ())), preferred_element_type=F32)


def block(*shape):
    return pl.BlockSpec((1, *shape), lambda m, *_: (m,) + (0,) * len(shape))


CHAINS = ((0, 0), (1, 0), (2, 0), (0, 1))
LIST = 7
THIRD = 2 * M
CHAIN = THIRD + 2 * LIST
OWN = len(CHAINS) * CHAIN
SIDE = OWN + LIST
CORE = SIDE + 3
TABLE = CORE + 1
SIZES = ((2, 5), (3, M), (M, M))


def table_kernel(owner_ref, out_ref, tier_ref):
    def clear(i, carry):
        out_ref[i] = 0
        return carry

    lax.fori_loop(0, TABLE, clear, 0)
    owners = [owner_ref[m % 2, m // 2] for m in range(M)]
    corner = [[BITS[d](v) for v in owners] for d in range(3)]
    at, over = lax.axis_index("dp"), lax.axis_index("fsdp")
    row = [BITS[d](at) for d in range(3)]
    column = [BITS[d](over >> 1) for d in range(3)]
    for c, (turn, axis) in enumerate(CHAINS):
        seen = [jnp.int32(0)] * 5
        spot = jnp.int32(0)
        for m in range(M):
            away = [corner[(turn + e) % 3][m] ^ row[(turn + e) % 3] for e in range(3)]
            if axis:
                away = [away[e] ^ column[(turn + e) % 3] for e in range(3)]
            array = jnp.where(away[2] == 1, 4, away[0] + 2 * away[1])
            slot = seen[0]
            for k in range(1, 5):
                slot = jnp.where(array == k, seen[k], slot)
            seen = [seen[k] + (array == k).astype(jnp.int32) for k in range(5)]
            out_ref[c * CHAIN + m] = array
            out_ref[c * CHAIN + M + m] = slot
            here = jnp.where(array < 4, spot, LIST - 1)
            out_ref[c * CHAIN + THIRD + here] = array
            out_ref[c * CHAIN + THIRD + LIST + here] = slot
            spot = spot + (array < 4).astype(jnp.int32)
            if c == 0:
                out_ref[OWN + jnp.where(array == 0, slot, LIST - 1)] = m
    for d in range(3):
        out_ref[SIDE + d] = row[d]
    node, face = jnp.int32(0), jnp.int32(0)
    for m in range(M):
        same = [[(corner[d][m] == corner[d][n]).astype(jnp.int32) for n in range(M)] for d in range(3)]
        node = jnp.maximum(node, sum(same[0][n] * same[1][n] * same[2][n] for n in range(M)))
        for d in range(3):
            face = jnp.maximum(face, sum(same[d]))
    tier = jnp.int32(len(SIZES) - 1)
    for k in range(len(SIZES) - 2, -1, -1):
        tier = jnp.where((node <= SIZES[k][0]) & (face <= SIZES[k][1]), k, tier)
    out_ref[CORE] = over & 1
    tier_ref[0] = tier


def make_tables(owner):
    smem = pl.BlockSpec(memory_space=pltpu.SMEM)
    return pl.pallas_call(
        table_kernel,
        out_shape=[jax.ShapeDtypeStruct((n,), jnp.int32) for n in (TABLE, 1)],
        in_specs=[smem],
        out_specs=[smem, smem],
        name="tables",
    )(owner)


HALVES = [(t, other) for other in (True, False) for t in range(3)]


def pack_kernel(table_ref, *refs):
    columns = refs[13]
    row = jnp.concatenate([refs[6][0, 0], jnp.zeros((1, 32), F32)], axis=1)
    lines = [row] + [pltpu.roll(row, WIDE - BO * o, 1) for o in (1, 2)]
    columns[...] = jnp.concatenate([x[:, 0:384] for x in lines] + [jnp.zeros((5, 384), F32)], axis=0).T
    for k, (t, other) in enumerate(HALVES):
        side = table_ref[SIDE + t]
        start = 2 * PIECE * t + PIECE * (1 - side if other else side)
        refs[7 + k][0, :, 0:864] = refs[k][0]
        refs[7 + k][0, :, 864:872] = columns[pl.ds(pl.multiple_of(start, PIECE), PIECE), :]
        refs[7 + k][0, :, 872:WIDE] = jnp.zeros((PIECE, 24), F32)


def pack(table, basis, eig, slots):
    def rows(t, other):
        def place(j, table):
            side = table[SIDE + t]
            return table[OWN + j], 2 * t + (1 - side if other else side), 0

        return pl.BlockSpec((1, PIECE, 864), place)

    out = pl.pallas_call(
        pack_kernel,
        out_shape=[jax.ShapeDtypeStruct((slots, PIECE, WIDE), F32)] * 6,
        grid_spec=pltpu.PrefetchScalarGridSpec(
            num_scalar_prefetch=1,
            grid=(slots,),
            in_specs=[rows(*half) for half in HALVES]
            + [pl.BlockSpec((1, 1, 1, 864), lambda j, table: (table[OWN + j] // 2, table[OWN + j] % 2, 0, 0))],
            out_specs=[block(PIECE, WIDE)] * 6,
            scratch_shapes=[pltpu.VMEM((384, 8), F32)],
        ),
        cost_estimate=pl.CostEstimate(flops=0, bytes_accessed=2_000_000 * slots, transcendentals=0),
        name="pack",
    )(table, *[basis] * 6, eig)
    return out[:3], out[3:]


ANY = pl.BlockSpec(memory_space=pl.ANY)
SMEM = pl.BlockSpec(memory_space=pltpu.SMEM)
VMEM = pl.BlockSpec(memory_space=pltpu.VMEM)


def gather_kernel(slots, table_ref, basis_ref, eig_ref, out_ref, sems):
    copies = []
    for j in range(slots):
        copies.append(pltpu.make_async_copy(basis_ref.at[table_ref[OWN + j]], out_ref.at[j, pl.ds(0, 320)], sems.at[j]))
    for copy in copies:
        copy.start()
    for j in range(slots):
        m = table_ref[OWN + j]
        line = jnp.concatenate([eig_ref[m // 2, m % 2], jnp.zeros((1, 64), F32)], axis=1)
        line = jnp.where(table_ref[CORE] == 0, line, pltpu.roll(line, 64, 1))
        rows = [line[:, 128 * k : 128 * (k + 1)] for k in range(3)]
        out_ref[j, 320:IN_ROWS, :] = jnp.concatenate(rows + [jnp.zeros((13, 128), F32)], axis=0)
    for copy in copies:
        copy.wait()


def gather_own(table, basis, eig, slots):
    return pl.pallas_call(
        functools.partial(gather_kernel, slots),
        out_shape=jax.ShapeDtypeStruct((slots, IN_ROWS, 128), F32),
        in_specs=[SMEM, ANY, VMEM],
        out_specs=VMEM,
        scratch_shapes=[pltpu.SemaphoreType.DMA((slots,))],
        cost_estimate=pl.CostEstimate(flops=0, bytes_accessed=400_000 * slots, transcendentals=0),
        name="gather",
    )(table, basis, eig)


def route_kernel(chains, slots, count, parts, table_ref, *refs):
    sources, outs, sems = refs[: count * len(chains)], refs[count * len(chains) : -1], refs[-1]
    each = slots // parts
    for i, c in enumerate(chains):
        for j in range(slots):
            base = c * CHAIN + (THIRD + j if count == 4 else j)
            array, slot = table_ref[base], table_ref[base + (LIST if count == 4 else M)]
            for k in range(count):

                @pl.when(array == k)
                def _():
                    out = outs[parts * i + j // each].at[j % each]
                    pltpu.make_async_copy(sources[count * i + k].at[slot], out, sems.at[i * slots + j]).start()

    for i in range(len(chains)):
        for j in range(slots):
            out = outs[parts * i + j // each].at[j % each]
            pltpu.make_async_copy(out, out, sems.at[i * slots + j]).wait()


def route(table, chains, slots, sources, shape, parts=1):
    count = len(sources[0])
    flat = [x for chain in sources for x in chain]
    return pl.pallas_call(
        functools.partial(route_kernel, chains, slots, count, parts),
        out_shape=[jax.ShapeDtypeStruct((slots // parts, *shape), F32)] * (parts * len(chains)),
        in_specs=[SMEM] + [ANY] * len(flat),
        out_specs=[VMEM] * (parts * len(chains)),
        scratch_shapes=[pltpu.SemaphoreType.DMA((len(chains) * slots,))],
        cost_estimate=pl.CostEstimate(flops=0, bytes_accessed=400_000 * slots, transcendentals=0),
        name="route",
    )(table, *flat)


def join_left(table_ref, mine, other, whole, a_scratch):
    core0 = table_ref[CORE] == 0
    for k in range(PARTS):

        @pl.when(pl.program_id(0) // (M // PARTS) == k)
        def _():
            low = jnp.where(core0, mine[k][0], other[k][0])
            high = jnp.where(core0, other[k][0], mine[k][0])
            whole[0:320, :] = low[0:320]
            whole[320:640, :] = high[0:320]
            a_scratch[0:2, :] = low[320:322]
            a_scratch[2:3, :] = low[322:323] + high[320:321]
            a_scratch[3:5, :] = high[321:323]


def doubled(value):
    high, low = split(value)
    both = jnp.concatenate([high, low], axis=1)
    return jnp.concatenate([both, both], axis=0)


def half_chain(grad_ref, pieces, whole, a_scratch, basis, turned, back, scaled):
    eigs = []
    for o in range(3):
        window = jnp.concatenate([ref[0, :, 256 * o : 256 * o + 384] for ref in pieces], axis=0)
        if o:
            window = pltpu.roll(window, 384 - 32 * o, 1)
        high, low = split(window[:, 0:BO])
        basis[o, 0:HALF, :] = high
        basis[o, HALF : 2 * HALF, :] = low
        back[o, 0:HALF, :] = high
        back[o, HALF : 2 * HALF, :] = high
        back[o, 2 * HALF : 3 * HALF, :] = low
        eigs.append(jnp.concatenate([ref[0, :, 768:WIDE][:, 96 + o : 97 + o] for ref in pieces], axis=0))

    for o in range(3):
        product = dot(basis[o], grad_ref[0, BO * o : BO * (o + 1), :])
        high, low = split(product[0:HALF] + product[HALF : 2 * HALF])
        for i in range(5):
            turned[i, HALF * o : HALF * (o + 1), 0:128] = high[:, BI * i : BI * (i + 1)]
            turned[i, HALF * o : HALF * (o + 1), 128:256] = low[:, BI * i : BI * (i + 1)]

    for i in range(5):
        product = dot(turned[i], doubled(whole[BI * i : BI * (i + 1), :]))
        rotated = product[:, 0:128] + product[:, 128:256]
        columns = slice(BI * i, BI * (i + 1))
        for o in range(3):
            part = rotated[HALF * o : HALF * (o + 1)] / (eigs[o] * a_scratch[i : i + 1, :] + damping)
            high, low = split(part)
            scaled[o, 0:HALF, columns] = high
            scaled[o, HALF : 2 * HALF, columns] = low
            scaled[o, 2 * HALF : 3 * HALF, columns] = high

    for o in range(3):
        yield o, dot_tn(back[o], scaled[o])


def mine_kernel(table_ref, grad_ref, p0, p1, p2, *refs):
    left, across, (out_ref, *scratch) = refs[:PARTS], refs[PARTS : 2 * PARTS], refs[2 * PARTS :]
    join_left(table_ref, left, across, *scratch[:2])
    for o, value in half_chain(grad_ref, (p0, p1, p2), *scratch):
        out_ref[0, BO * o : BO * (o + 1), :] = value


def other_kernel(table_ref, grad_ref, p0, p1, p2, *refs):
    left, across, (part_ref, out_ref, *scratch, whole) = refs[:PARTS], refs[PARTS : 2 * PARTS], refs[2 * PARTS :]
    join_left(table_ref, left, across, *scratch[:2])
    for o, value in half_chain(grad_ref, (p0, p1, p2), *scratch):
        rows = slice(BO * o, BO * (o + 1))
        high, low = split(value + part_ref[0, rows, :])
        for i in range(5):
            whole[i, rows, 0:128] = high[:, BI * i : BI * (i + 1)]
            whole[i, rows, 128:256] = low[:, BI * i : BI * (i + 1)]
    for i in range(5):
        product = dot(whole[i], doubled(scratch[0][BI * i : BI * (i + 1), :].T))
        out_ref[0, :, BI * i : BI * (i + 1)] = (product[:, 0:128] + product[:, 128:256]).astype(BF16)


CHAIN_SCRATCH = [
    pltpu.VMEM((640, 128), F32),
    pltpu.VMEM((8, 128), F32),
    pltpu.VMEM((3, 2 * HALF, BO), BF16),
    pltpu.VMEM((5, 3 * HALF, 256), BF16),
    pltpu.VMEM((3, 3 * HALF, BO), BF16),
    pltpu.VMEM((3, 3 * HALF, 640), BF16),
]
def part_block(k):
    each = M // PARTS
    return pl.BlockSpec((1, IN_ROWS, 128), lambda m, *_: (jnp.clip(m - each * k, 0, each - 1), 0, 0))


CHAIN_IN = [block(864, 640)] + [block(PIECE, WIDE)] * 3 + [part_block(k) for k in range(PARTS)] * 2


def chain_mine(table, grads, pieces, left):
    return pl.pallas_call(
        mine_kernel,
        out_shape=jax.ShapeDtypeStruct((M, 864, 640), F32),
        grid_spec=pltpu.PrefetchScalarGridSpec(
            num_scalar_prefetch=1,
            grid=(M,),
            in_specs=CHAIN_IN,
            out_specs=block(864, 640),
            scratch_shapes=CHAIN_SCRATCH,
        ),
        compiler_params=PARAMS,
        cost_estimate=pl.CostEstimate(flops=1_000_000, bytes_accessed=1_000_000, transcendentals=0),
        name="mine",
    )(table, grads, *pieces, *left)


def chain_other(table, grads, pieces, left, part):
    return pl.pallas_call(
        other_kernel,
        out_shape=jax.ShapeDtypeStruct((M, 864, 640), BF16),
        grid_spec=pltpu.PrefetchScalarGridSpec(
            num_scalar_prefetch=1,
            grid=(M,),
            in_specs=CHAIN_IN + [block(864, 640)],
            out_specs=block(864, 640),
            scratch_shapes=CHAIN_SCRATCH + [pltpu.VMEM((5, 864, 256), BF16)],
        ),
        compiler_params=PARAMS,
        cost_estimate=pl.CostEstimate(flops=20_000_000_000, bytes_accessed=40_000_000, transcendentals=0),
        name="other",
    )(table, grads, *pieces, *left, part)


def exchange(x, axis, d):
    if axis == "dp":
        pairs = [(v, SWAPS[d % 3](v)) for v in range(8)]
    else:
        pairs = [(f, 2 * SWAPS[d](f >> 1) + (f & 1)) for f in range(16)]
    return lax.ppermute(x, axis, pairs)


def apart(v, w):
    bits = [f(v) ^ f(w) for f in BITS]
    return next(u for u in range(8) if [f(u) for f in BITS] == bits)


def together(arrays):
    return list(lax.optimization_barrier(tuple(arrays)))


def precondition(sizes, table, grads, basis_in, eig_in, basis, eig_out):
    both = ("dp", "fsdp")
    every = [(d, q, c) for d in range(8) for q in range(8) for c in range(2)]
    inner = gather_own(table, basis_in, eig_in, sizes[0])
    inner = lax.ppermute(inner, both, [(d * 16 + q * 2 + c, d * 16 + 2 * apart(d, q) + c) for d, q, c in every])
    inner = lax.ppermute(inner, both, [(d * 16 + q * 2 + c, apart(d, q) * 16 + q * 2 + c) for d, q, c in every])

    shape, in_shape = (PIECE, WIDE), (IN_ROWS, 128)
    send, keep = pack(table, basis, eig_out, sizes[0])
    first = [exchange(send[t], "dp", t) for t in range(3)]
    second = [exchange(keep[t], "dp", t + 1) for t in range(3)]
    first = together(first)
    follow = [exchange(first[t], "dp", t + 1) for t in range(3)]
    in_first = exchange(inner, "fsdp", 0)
    in_second = exchange(inner, "fsdp", 1)
    arrived = together([*second, *follow])
    held = [[keep[t], first[t], arrived[t], arrived[3 + t]] for t in range(3)]
    send = route(table, (0, 1, 2), sizes[1], held, shape)
    third = [exchange(send[t], "dp", t + 2) for t in range(3)]
    in_first = together([in_first, *send])[0]
    in_follow = exchange(in_first, "fsdp", 1)
    in_held = [inner, in_first, in_second, in_follow]
    in_third = exchange(route(table, (3,), sizes[1], [in_held], in_shape)[0], "fsdp", 2)
    third = together(third)
    send = route(table, (0, 1, 2), M, [[*held[t], third[t]] for t in range(3)], shape)
    rest = [exchange(send[t], "dp", t) for t in range(3)]
    in_third = together([in_third, *send])[0]
    left = list(route(table, (3,), M, [[*in_held, in_third]], in_shape, PARTS))
    left += [lax.ppermute(x, "fsdp", [(f, f ^ 1) for f in range(16)]) for x in left]
    part = chain_mine(table, grads, send, left)
    return chain_other(table, grads, rest, left, part)


def shards(grads, basis_in, eig_in, basis_out, eig_out, owner):
    table, tier = make_tables(jnp.swapaxes(owner, 0, 1))
    arrays = (
        table,
        jnp.swapaxes(grads.reshape(M, 640, 864), 1, 2),
        basis_in.reshape(M, 320, 128),
        eig_in,
        jnp.swapaxes(basis_out.reshape(M, 864, BO), 1, 2),
        eig_out,
    )
    plans = [functools.partial(precondition, sizes) for sizes in SIZES]
    result = lax.switch(tier.reshape(()), plans, *arrays)
    return jnp.swapaxes(result, 1, 2).reshape(grads.shape)


def solution(mesh):
    placed = (
        P(None, None, "dp", "fsdp"),
        P(None, None, "dp", "fsdp", None),
        P(None, None, "dp", "fsdp"),
        P(None, None, "dp", "fsdp", None),
        P(None, None, "dp", "fsdp"),
        P(),
    )
    return jax.shard_map(
        shards, mesh=mesh, in_specs=placed, out_specs=P(None, None, "dp", "fsdp"), check_vma=False
    )
```

```python
import functools

import jax
import jax.numpy as jnp
from jax import lax
from jax.experimental import pallas as pl
from jax.experimental.pallas import tpu as pltpu
from jax.sharding import PartitionSpec as P

BI = 128
BO = 288
M = 6
damping = 0.1
PARAMS = pltpu.CompilerParams(vmem_limit_bytes=62 * 2**20)
F32 = jnp.float32
BF16 = jnp.bfloat16

PIECE = 48
WIDE = 896
HALF = 3 * PIECE
IN_ROWS = 336
PARTS = 3

BITS = (lambda v: v >> 2, lambda v: (v ^ (v >> 1)) & 1, lambda v: (v & 3) >> 1)
SWAPS = (lambda v: v ^ 4, lambda v: v ^ 1, lambda v: (v & 4) | (3 - (v & 3)))


def split(x):
    high = x.astype(BF16)
    return high, (x - high.astype(F32)).astype(BF16)


def dot(a, b):
    return jnp.dot(a, b, preferred_element_type=F32)


def dot_tn(a, b):
    return lax.dot_general(a, b, (((0,), (0,)), ((), ())), preferred_element_type=F32)


def block(*shape):
    return pl.BlockSpec((1, *shape), lambda m, *_: (m,) + (0,) * len(shape))


CHAINS = ((0, 0), (1, 0), (2, 0), (0, 1))
LIST = 7
THIRD = 2 * M
CHAIN = THIRD + 2 * LIST
OWN = len(CHAINS) * CHAIN
SIDE = OWN + LIST
CORE = SIDE + 3
TABLE = CORE + 1
SIZES = ((2, 5), (3, M), (M, M))


def table_kernel(owner_ref, out_ref, tier_ref):
    def clear(i, carry):
        out_ref[i] = 0
        return carry

    lax.fori_loop(0, TABLE, clear, 0)
    owners = [owner_ref[m % 2, m // 2] for m in range(M)]
    corner = [[BITS[d](v) for v in owners] for d in range(3)]
    at, over = lax.axis_index("dp"), lax.axis_index("fsdp")
    row = [BITS[d](at) for d in range(3)]
    column = [BITS[d](over >> 1) for d in range(3)]
    for c, (turn, axis) in enumerate(CHAINS):
        seen = [jnp.int32(0)] * 5
        spot = jnp.int32(0)
        for m in range(M):
            away = [corner[(turn + e) % 3][m] ^ row[(turn + e) % 3] for e in range(3)]
            if axis:
                away = [away[e] ^ column[(turn + e) % 3] for e in range(3)]
            array = jnp.where(away[2] == 1, 4, away[0] + 2 * away[1])
            slot = seen[0]
            for k in range(1, 5):
                slot = jnp.where(array == k, seen[k], slot)
            seen = [seen[k] + (array == k).astype(jnp.int32) for k in range(5)]
            out_ref[c * CHAIN + m] = array
            out_ref[c * CHAIN + M + m] = slot
            here = jnp.where(array < 4, spot, LIST - 1)
            out_ref[c * CHAIN + THIRD + here] = array
            out_ref[c * CHAIN + THIRD + LIST + here] = slot
            spot = spot + (array < 4).astype(jnp.int32)
            if c == 0:
                out_ref[OWN + jnp.where(array == 0, slot, LIST - 1)] = m
    for d in range(3):
        out_ref[SIDE + d] = row[d]
    node, face = jnp.int32(0), jnp.int32(0)
    for m in range(M):
        same = [[(corner[d][m] == corner[d][n]).astype(jnp.int32) for n in range(M)] for d in range(3)]
        node = jnp.maximum(node, sum(same[0][n] * same[1][n] * same[2][n] for n in range(M)))
        for d in range(3):
            face = jnp.maximum(face, sum(same[d]))
    tier = jnp.int32(len(SIZES) - 1)
    for k in range(len(SIZES) - 2, -1, -1):
        tier = jnp.where((node <= SIZES[k][0]) & (face <= SIZES[k][1]), k, tier)
    out_ref[CORE] = over & 1
    tier_ref[0] = tier


def make_tables(owner):
    smem = pl.BlockSpec(memory_space=pltpu.SMEM)
    return pl.pallas_call(
        table_kernel,
        out_shape=[jax.ShapeDtypeStruct((n,), jnp.int32) for n in (TABLE, 1)],
        in_specs=[smem],
        out_specs=[smem, smem],
        name="tables",
    )(owner)


HALVES = [(t, other) for other in (True, False) for t in range(3)]


def pack_kernel(table_ref, *refs):
    columns = refs[13]
    row = jnp.concatenate([refs[6][0, 0], jnp.zeros((1, 32), F32)], axis=1)
    lines = [row] + [pltpu.roll(row, WIDE - BO * o, 1) for o in (1, 2)]
    columns[...] = jnp.concatenate([x[:, 0:384] for x in lines] + [jnp.zeros((5, 384), F32)], axis=0).T
    for k, (t, other) in enumerate(HALVES):
        side = table_ref[SIDE + t]
        start = 2 * PIECE * t + PIECE * (1 - side if other else side)
        refs[7 + k][0, :, 0:864] = refs[k][0]
        refs[7 + k][0, :, 864:872] = columns[pl.ds(pl.multiple_of(start, PIECE), PIECE), :]
        refs[7 + k][0, :, 872:WIDE] = jnp.zeros((PIECE, 24), F32)


def pack(table, basis, eig, slots):
    def rows(t, other):
        def place(j, table):
            side = table[SIDE + t]
            return table[OWN + j], 2 * t + (1 - side if other else side), 0

        return pl.BlockSpec((1, PIECE, 864), place)

    out = pl.pallas_call(
        pack_kernel,
        out_shape=[jax.ShapeDtypeStruct((slots, PIECE, WIDE), F32)] * 6,
        grid_spec=pltpu.PrefetchScalarGridSpec(
            num_scalar_prefetch=1,
            grid=(slots,),
            in_specs=[rows(*half) for half in HALVES]
            + [pl.BlockSpec((1, 1, 1, 864), lambda j, table: (table[OWN + j] // 2, table[OWN + j] % 2, 0, 0))],
            out_specs=[block(PIECE, WIDE)] * 6,
            scratch_shapes=[pltpu.VMEM((384, 8), F32)],
        ),
        cost_estimate=pl.CostEstimate(flops=0, bytes_accessed=2_000_000 * slots, transcendentals=0),
        name="pack",
    )(table, *[basis] * 6, eig)
    return out[:3], out[3:]


ANY = pl.BlockSpec(memory_space=pl.ANY)
SMEM = pl.BlockSpec(memory_space=pltpu.SMEM)
VMEM = pl.BlockSpec(memory_space=pltpu.VMEM)


def gather_kernel(slots, table_ref, basis_ref, eig_ref, out_ref, sems):
    copies = []
    for j in range(slots):
        copies.append(pltpu.make_async_copy(basis_ref.at[table_ref[OWN + j]], out_ref.at[j, pl.ds(0, 320)], sems.at[j]))
    for copy in copies:
        copy.start()
    for j in range(slots):
        m = table_ref[OWN + j]
        line = jnp.concatenate([eig_ref[m // 2, m % 2], jnp.zeros((1, 64), F32)], axis=1)
        line = jnp.where(table_ref[CORE] == 0, line, pltpu.roll(line, 64, 1))
        rows = [line[:, 128 * k : 128 * (k + 1)] for k in range(3)]
        out_ref[j, 320:IN_ROWS, :] = jnp.concatenate(rows + [jnp.zeros((13, 128), F32)], axis=0)
    for copy in copies:
        copy.wait()


def gather_own(table, basis, eig, slots):
    return pl.pallas_call(
        functools.partial(gather_kernel, slots),
        out_shape=jax.ShapeDtypeStruct((slots, IN_ROWS, 128), F32),
        in_specs=[SMEM, ANY, VMEM],
        out_specs=VMEM,
        scratch_shapes=[pltpu.SemaphoreType.DMA((slots,))],
        cost_estimate=pl.CostEstimate(flops=0, bytes_accessed=400_000 * slots, transcendentals=0),
        name="gather",
    )(table, basis, eig)


def route_kernel(chains, slots, count, parts, table_ref, *refs):
    sources, outs, sems = refs[: count * len(chains)], refs[count * len(chains) : -1], refs[-1]
    each = slots // parts
    for i, c in enumerate(chains):
        for j in range(slots):
            base = c * CHAIN + (THIRD + j if count == 4 else j)
            array, slot = table_ref[base], table_ref[base + (LIST if count == 4 else M)]
            for k in range(count):

                @pl.when(array == k)
                def _():
                    out = outs[parts * i + j // each].at[j % each]
                    pltpu.make_async_copy(sources[count * i + k].at[slot], out, sems.at[i * slots + j]).start()

    for i in range(len(chains)):
        for j in range(slots):
            out = outs[parts * i + j // each].at[j % each]
            pltpu.make_async_copy(out, out, sems.at[i * slots + j]).wait()


def route(table, chains, slots, sources, shape, parts=1):
    count = len(sources[0])
    flat = [x for chain in sources for x in chain]
    return pl.pallas_call(
        functools.partial(route_kernel, chains, slots, count, parts),
        out_shape=[jax.ShapeDtypeStruct((slots // parts, *shape), F32)] * (parts * len(chains)),
        in_specs=[SMEM] + [ANY] * len(flat),
        out_specs=[VMEM] * (parts * len(chains)),
        scratch_shapes=[pltpu.SemaphoreType.DMA((len(chains) * slots,))],
        cost_estimate=pl.CostEstimate(flops=0, bytes_accessed=400_000 * slots, transcendentals=0),
        name="route",
    )(table, *flat)


def join_left(table_ref, mine, other, whole, a_scratch):
    core = table_ref[CORE]
    for k in range(PARTS):

        @pl.when(pl.program_id(0) // (M // PARTS) == k)
        def _():
            for half, at in ((mine, core), (other, 1 - core)):
                whole[pl.ds(pl.multiple_of(320 * at, 8), 320), :] = half[k][0, 0:320]
            low = jnp.where(core == 0, mine[k][0, 320:328], other[k][0, 320:328])
            high = jnp.where(core == 0, other[k][0, 320:328], mine[k][0, 320:328])
            a_scratch[0:2, :] = low[0:2]
            a_scratch[2:3, :] = low[2:3] + high[0:1]
            a_scratch[3:5, :] = high[1:3]


def doubled(value):
    high, low = split(value)
    both = jnp.concatenate([high, low], axis=1)
    return jnp.concatenate([both, both], axis=0)


def half_chain(grad_ref, pieces, whole, a_scratch, basis, turned, back, scaled):
    eigs = []
    for o in range(3):
        window = jnp.concatenate([ref[0, :, 256 * o : 256 * o + 384] for ref in pieces], axis=0)
        if o:
            window = pltpu.roll(window, 384 - 32 * o, 1)
        high, low = split(window[:, 0:BO])
        basis[o, 0:HALF, :] = high
        basis[o, HALF : 2 * HALF, :] = low
        back[o, 0:HALF, :] = high
        back[o, HALF : 2 * HALF, :] = high
        back[o, 2 * HALF : 3 * HALF, :] = low
        eigs.append(jnp.concatenate([ref[0, :, 768:WIDE][:, 96 + o : 97 + o] for ref in pieces], axis=0))

    for o in range(3):
        product = dot(basis[o], grad_ref[0, BO * o : BO * (o + 1), :])
        high, low = split(product[0:HALF] + product[HALF : 2 * HALF])
        for i in range(5):
            turned[i, HALF * o : HALF * (o + 1), 0:128] = high[:, BI * i : BI * (i + 1)]
            turned[i, HALF * o : HALF * (o + 1), 128:256] = low[:, BI * i : BI * (i + 1)]

    for i in range(5):
        product = dot(turned[i], doubled(whole[BI * i : BI * (i + 1), :]))
        rotated = product[:, 0:128] + product[:, 128:256]
        columns = slice(BI * i, BI * (i + 1))
        for o in range(3):
            part = rotated[HALF * o : HALF * (o + 1)] / (eigs[o] * a_scratch[i : i + 1, :] + damping)
            high, low = split(part)
            scaled[o, 0:HALF, columns] = high
            scaled[o, HALF : 2 * HALF, columns] = low
            scaled[o, 2 * HALF : 3 * HALF, columns] = high

    for o in range(3):
        yield o, dot_tn(back[o], scaled[o])


def mine_kernel(table_ref, grad_ref, p0, p1, p2, *refs):
    left, across, (out_ref, *scratch) = refs[:PARTS], refs[PARTS : 2 * PARTS], refs[2 * PARTS :]
    join_left(table_ref, left, across, *scratch[:2])
    for o, value in half_chain(grad_ref, (p0, p1, p2), *scratch):
        out_ref[0, BO * o : BO * (o + 1), :] = value


def other_kernel(table_ref, grad_ref, p0, p1, p2, *refs):
    left, across, (part_ref, out_ref, *scratch, whole) = refs[:PARTS], refs[PARTS : 2 * PARTS], refs[2 * PARTS :]
    join_left(table_ref, left, across, *scratch[:2])
    for o, value in half_chain(grad_ref, (p0, p1, p2), *scratch):
        rows = slice(BO * o, BO * (o + 1))
        high, low = split(value + part_ref[0, rows, :])
        for i in range(5):
            whole[i, rows, 0:128] = high[:, BI * i : BI * (i + 1)]
            whole[i, rows, 128:256] = low[:, BI * i : BI * (i + 1)]
    for i in range(5):
        product = dot(whole[i], doubled(scratch[0][BI * i : BI * (i + 1), :].T))
        out_ref[0, :, BI * i : BI * (i + 1)] = (product[:, 0:128] + product[:, 128:256]).astype(BF16)


CHAIN_SCRATCH = [
    pltpu.VMEM((640, 128), F32),
    pltpu.VMEM((8, 128), F32),
    pltpu.VMEM((3, 2 * HALF, BO), BF16),
    pltpu.VMEM((5, 3 * HALF, 256), BF16),
    pltpu.VMEM((3, 3 * HALF, BO), BF16),
    pltpu.VMEM((3, 3 * HALF, 640), BF16),
]
def part_block(k):
    each = M // PARTS
    return pl.BlockSpec((1, IN_ROWS, 128), lambda m, *_: (jnp.clip(m - each * k, 0, each - 1), 0, 0))


CHAIN_IN = [block(864, 640)] + [block(PIECE, WIDE)] * 3 + [part_block(k) for k in range(PARTS)] * 2


def chain_mine(table, grads, pieces, left):
    return pl.pallas_call(
        mine_kernel,
        out_shape=jax.ShapeDtypeStruct((M, 864, 640), F32),
        grid_spec=pltpu.PrefetchScalarGridSpec(
            num_scalar_prefetch=1,
            grid=(M,),
            in_specs=CHAIN_IN,
            out_specs=block(864, 640),
            scratch_shapes=CHAIN_SCRATCH,
        ),
        compiler_params=PARAMS,
        cost_estimate=pl.CostEstimate(flops=1_000_000, bytes_accessed=1_000_000, transcendentals=0),
        name="mine",
    )(table, grads, *pieces, *left)


def chain_other(table, grads, pieces, left, part):
    return pl.pallas_call(
        other_kernel,
        out_shape=jax.ShapeDtypeStruct((M, 864, 640), BF16),
        grid_spec=pltpu.PrefetchScalarGridSpec(
            num_scalar_prefetch=1,
            grid=(M,),
            in_specs=CHAIN_IN + [block(864, 640)],
            out_specs=block(864, 640),
            scratch_shapes=CHAIN_SCRATCH + [pltpu.VMEM((5, 864, 256), BF16)],
        ),
        compiler_params=PARAMS,
        cost_estimate=pl.CostEstimate(flops=20_000_000_000, bytes_accessed=40_000_000, transcendentals=0),
        name="other",
    )(table, grads, *pieces, *left, part)


def exchange(x, axis, d):
    if axis == "dp":
        pairs = [(v, SWAPS[d % 3](v)) for v in range(8)]
    else:
        pairs = [(f, 2 * SWAPS[d](f >> 1) + (f & 1)) for f in range(16)]
    return lax.ppermute(x, axis, pairs)


def apart(v, w):
    bits = [f(v) ^ f(w) for f in BITS]
    return next(u for u in range(8) if [f(u) for f in BITS] == bits)


def together(arrays):
    return list(lax.optimization_barrier(tuple(arrays)))


def precondition(sizes, table, grads, basis_in, eig_in, basis, eig_out):
    both = ("dp", "fsdp")
    every = [(d, q, c) for d in range(8) for q in range(8) for c in range(2)]
    inner = gather_own(table, basis_in, eig_in, sizes[0])
    inner = lax.ppermute(inner, both, [(d * 16 + q * 2 + c, d * 16 + 2 * apart(d, q) + c) for d, q, c in every])
    inner = lax.ppermute(inner, both, [(d * 16 + q * 2 + c, apart(d, q) * 16 + q * 2 + c) for d, q, c in every])

    shape, in_shape = (PIECE, WIDE), (IN_ROWS, 128)
    send, keep = pack(table, basis, eig_out, sizes[0])
    first = [exchange(send[t], "dp", t) for t in range(3)]
    second = [exchange(keep[t], "dp", t + 1) for t in range(3)]
    first = together(first)
    follow = [exchange(first[t], "dp", t + 1) for t in range(3)]
    in_first = exchange(inner, "fsdp", 0)
    in_second = exchange(inner, "fsdp", 1)
    arrived = together([*second, *follow])
    held = [[keep[t], first[t], arrived[t], arrived[3 + t]] for t in range(3)]
    send = route(table, (0, 1, 2), sizes[1], held, shape)
    third = [exchange(send[t], "dp", t + 2) for t in range(3)]
    in_first = together([in_first, *send])[0]
    in_follow = exchange(in_first, "fsdp", 1)
    in_held = [inner, in_first, in_second, in_follow]
    in_third = exchange(route(table, (3,), sizes[1], [in_held], in_shape)[0], "fsdp", 2)
    third = together(third)
    send = route(table, (0, 1, 2), M, [[*held[t], third[t]] for t in range(3)], shape)
    rest = [exchange(send[t], "dp", t) for t in range(3)]
    in_third = together([in_third, *send])[0]
    left = list(route(table, (3,), M, [[*in_held, in_third]], in_shape, PARTS))
    left += [lax.ppermute(x, "fsdp", [(f, f ^ 1) for f in range(16)]) for x in left]
    return chain_mine(table, grads, send, left), rest, left


def shards(grads, basis_in, eig_in, basis_out, eig_out, owner):
    table, tier = make_tables(jnp.swapaxes(owner, 0, 1))
    arrays = (
        table,
        jnp.swapaxes(grads.reshape(M, 640, 864), 1, 2),
        basis_in.reshape(M, 320, 128),
        eig_in,
        jnp.swapaxes(basis_out.reshape(M, 864, BO), 1, 2),
        eig_out,
    )
    plans = [functools.partial(precondition, sizes) for sizes in SIZES]
    part, rest, left = lax.switch(tier.reshape(()), plans, *arrays)
    result = chain_other(table, arrays[1], rest, left, part)
    return jnp.swapaxes(result, 1, 2).reshape(grads.shape)


def solution(mesh):
    placed = (
        P(None, None, "dp", "fsdp"),
        P(None, None, "dp", "fsdp", None),
        P(None, None, "dp", "fsdp"),
        P(None, None, "dp", "fsdp", None),
        P(None, None, "dp", "fsdp"),
        P(),
    )
    return jax.shard_map(
        shards, mesh=mesh, in_specs=placed, out_specs=P(None, None, "dp", "fsdp"), check_vma=False
    )
```

```python
import functools

import jax
import jax.numpy as jnp
from jax import lax
from jax.experimental import pallas as pl
from jax.experimental.pallas import tpu as pltpu
from jax.sharding import PartitionSpec as P

BI = 128
BO = 288
M = 6
damping = 0.1
PARAMS = pltpu.CompilerParams(vmem_limit_bytes=62 * 2**20)
F32 = jnp.float32
BF16 = jnp.bfloat16

PIECE = 48
WIDE = 896
HALF = 3 * PIECE
IN_ROWS = 336
PARTS = 3

BITS = (lambda v: v >> 2, lambda v: (v ^ (v >> 1)) & 1, lambda v: (v & 3) >> 1)
SWAPS = (lambda v: v ^ 4, lambda v: v ^ 1, lambda v: (v & 4) | (3 - (v & 3)))


def split(x):
    high = x.astype(BF16)
    return high, (x - high.astype(F32)).astype(BF16)


def dot(a, b):
    return jnp.dot(a, b, preferred_element_type=F32)


def dot_tn(a, b):
    return lax.dot_general(a, b, (((0,), (0,)), ((), ())), preferred_element_type=F32)


def block(*shape):
    return pl.BlockSpec((1, *shape), lambda m, *_: (m,) + (0,) * len(shape))


CHAINS = ((0, 1, 2, 0), (1, 2, 0, 0), (2, 0, 1, 0), (0, 2, 1, 1))
LIST = 7
THIRD = 2 * M
CHAIN = THIRD + 2 * LIST
OWN = len(CHAINS) * CHAIN
SIDE = OWN + LIST
CORE = SIDE + 3
TABLE = CORE + 1
SIZES = ((2, 5), (3, M), (M, M))


def table_kernel(owner_ref, out_ref, tier_ref):
    for start, length in [(c * CHAIN + THIRD, 2 * LIST) for c in range(len(CHAINS))] + [(OWN, LIST)]:
        for i in range(length):
            out_ref[start + i] = 0
    owners = [owner_ref[m % 2, m // 2] for m in range(M)]
    corner = [[BITS[d](v) for v in owners] for d in range(3)]
    at, over = lax.axis_index("dp"), lax.axis_index("fsdp")
    row = [BITS[d](at) for d in range(3)]
    column = [BITS[d](over >> 1) for d in range(3)]
    for c, (*order, axis) in enumerate(CHAINS):
        seen = [jnp.int32(0)] * 5
        spot = jnp.int32(0)
        for m in range(M):
            away = [corner[d][m] ^ row[d] for d in order]
            if axis:
                away = [away[e] ^ column[order[e]] for e in range(3)]
            array = jnp.where(away[2] == 1, 4, away[0] + 2 * away[1])
            slot = seen[0]
            for k in range(1, 5):
                slot = jnp.where(array == k, seen[k], slot)
            seen = [seen[k] + (array == k).astype(jnp.int32) for k in range(5)]
            out_ref[c * CHAIN + m] = array
            out_ref[c * CHAIN + M + m] = slot
            here = jnp.where(array < 4, spot, LIST - 1)
            out_ref[c * CHAIN + THIRD + here] = array
            out_ref[c * CHAIN + THIRD + LIST + here] = slot
            spot = spot + (array < 4).astype(jnp.int32)
            if c == 0:
                out_ref[OWN + jnp.where(array == 0, slot, LIST - 1)] = m
    for d in range(3):
        out_ref[SIDE + d] = row[d]
    node, face = jnp.int32(0), jnp.int32(0)
    for m in range(M):
        same = [[(corner[d][m] == corner[d][n]).astype(jnp.int32) for n in range(M)] for d in range(3)]
        node = jnp.maximum(node, sum(same[0][n] * same[1][n] * same[2][n] for n in range(M)))
        for d in range(3):
            face = jnp.maximum(face, sum(same[d]))
    tier = jnp.int32(len(SIZES) - 1)
    for k in range(len(SIZES) - 2, -1, -1):
        tier = jnp.where((node <= SIZES[k][0]) & (face <= SIZES[k][1]), k, tier)
    out_ref[CORE] = over & 1
    tier_ref[0] = tier


def make_tables(owner):
    smem = pl.BlockSpec(memory_space=pltpu.SMEM)
    return pl.pallas_call(
        table_kernel,
        out_shape=[jax.ShapeDtypeStruct((n,), jnp.int32) for n in (TABLE, 1)],
        in_specs=[smem],
        out_specs=[smem, smem],
        name="tables",
    )(owner)


HALVES = [(t, other) for other in (True, False) for t in range(3)]


def pack_kernel(table_ref, *refs):
    columns = refs[13]
    row = jnp.concatenate([refs[6][0, 0], jnp.zeros((1, 32), F32)], axis=1)
    lines = [row] + [pltpu.roll(row, WIDE - BO * o, 1) for o in (1, 2)]
    columns[...] = jnp.concatenate([x[:, 0:384] for x in lines] + [jnp.zeros((5, 384), F32)], axis=0).T
    for k, (t, other) in enumerate(HALVES):
        side = table_ref[SIDE + t]
        start = 2 * PIECE * t + PIECE * (1 - side if other else side)
        refs[7 + k][0, :, 0:864] = refs[k][0]
        refs[7 + k][0, :, 864:872] = columns[pl.ds(pl.multiple_of(start, PIECE), PIECE), :]
        refs[7 + k][0, :, 872:WIDE] = jnp.zeros((PIECE, 24), F32)


def pack(table, basis, eig, slots):
    def rows(t, other):
        def place(j, table):
            side = table[SIDE + t]
            return table[OWN + j], 2 * t + (1 - side if other else side), 0

        return pl.BlockSpec((1, PIECE, 864), place)

    out = pl.pallas_call(
        pack_kernel,
        out_shape=[jax.ShapeDtypeStruct((slots, PIECE, WIDE), F32)] * 6,
        grid_spec=pltpu.PrefetchScalarGridSpec(
            num_scalar_prefetch=1,
            grid=(slots,),
            in_specs=[rows(*half) for half in HALVES]
            + [pl.BlockSpec((1, 1, 1, 864), lambda j, table: (table[OWN + j] // 2, table[OWN + j] % 2, 0, 0))],
            out_specs=[block(PIECE, WIDE)] * 6,
            scratch_shapes=[pltpu.VMEM((384, 8), F32)],
        ),
        cost_estimate=pl.CostEstimate(flops=0, bytes_accessed=2_000_000 * slots, transcendentals=0),
        name="pack",
    )(table, *[basis] * 6, eig)
    return out[:3], out[3:]


ANY = pl.BlockSpec(memory_space=pl.ANY)
SMEM = pl.BlockSpec(memory_space=pltpu.SMEM)
VMEM = pl.BlockSpec(memory_space=pltpu.VMEM)


def gather_kernel(slots, table_ref, basis_ref, eig_ref, out_ref, sems):
    copies = []
    for j in range(slots):
        copies.append(pltpu.make_async_copy(basis_ref.at[table_ref[OWN + j]], out_ref.at[j, pl.ds(0, 320)], sems.at[j]))
    for copy in copies:
        copy.start()
    for j in range(slots):
        m = table_ref[OWN + j]
        line = jnp.concatenate([eig_ref[m // 2, m % 2], jnp.zeros((1, 64), F32)], axis=1)
        line = jnp.where(table_ref[CORE] == 0, line, pltpu.roll(line, 64, 1))
        rows = [line[:, 128 * k : 128 * (k + 1)] for k in range(3)]
        out_ref[j, 320:IN_ROWS, :] = jnp.concatenate(rows + [jnp.zeros((13, 128), F32)], axis=0)
    for copy in copies:
        copy.wait()


def gather_own(table, basis, eig, slots):
    return pl.pallas_call(
        functools.partial(gather_kernel, slots),
        out_shape=jax.ShapeDtypeStruct((slots, IN_ROWS, 128), F32),
        in_specs=[SMEM, ANY, VMEM],
        out_specs=VMEM,
        scratch_shapes=[pltpu.SemaphoreType.DMA((slots,))],
        cost_estimate=pl.CostEstimate(flops=0, bytes_accessed=400_000 * slots, transcendentals=0),
        name="gather",
    )(table, basis, eig)


def route_kernel(chains, slots, count, parts, table_ref, *refs):
    sources, outs, sems = refs[: count * len(chains)], refs[count * len(chains) : -1], refs[-1]
    each = slots // parts
    for i, c in enumerate(chains):
        for j in range(slots):
            base = c * CHAIN + (THIRD + j if count == 4 else j)
            array, slot = table_ref[base], table_ref[base + (LIST if count == 4 else M)]
            for k in range(count):

                @pl.when(array == k)
                def _():
                    out = outs[parts * i + j // each].at[j % each]
                    pltpu.make_async_copy(sources[count * i + k].at[slot], out, sems.at[i * slots + j]).start()

    for i in range(len(chains)):
        for j in range(slots):
            out = outs[parts * i + j // each].at[j % each]
            pltpu.make_async_copy(out, out, sems.at[i * slots + j]).wait()


def route(table, chains, slots, sources, shape, parts=1):
    count = len(sources[0])
    flat = [x for chain in sources for x in chain]
    return pl.pallas_call(
        functools.partial(route_kernel, chains, slots, count, parts),
        out_shape=[jax.ShapeDtypeStruct((slots // parts, *shape), F32)] * (parts * len(chains)),
        in_specs=[SMEM] + [ANY] * len(flat),
        out_specs=[VMEM] * (parts * len(chains)),
        scratch_shapes=[pltpu.SemaphoreType.DMA((len(chains) * slots,))],
        cost_estimate=pl.CostEstimate(flops=0, bytes_accessed=400_000 * slots, transcendentals=0),
        name="route",
    )(table, *flat)


def join_left(table_ref, mine, other, whole, a_scratch):
    core = table_ref[CORE]
    for k in range(PARTS):

        @pl.when(pl.program_id(0) // (M // PARTS) == k)
        def _():
            for half, at in ((mine, core), (other, 1 - core)):
                whole[pl.ds(pl.multiple_of(320 * at, 8), 320), :] = half[k][0, 0:320]
            low = jnp.where(core == 0, mine[k][0, 320:328], other[k][0, 320:328])
            high = jnp.where(core == 0, other[k][0, 320:328], mine[k][0, 320:328])
            a_scratch[0:2, :] = low[0:2]
            a_scratch[2:3, :] = low[2:3] + high[0:1]
            a_scratch[3:5, :] = high[1:3]


def doubled(value):
    high, low = split(value)
    both = jnp.concatenate([high, low], axis=1)
    return jnp.concatenate([both, both], axis=0)


def half_chain(grad_ref, pieces, whole, a_scratch, basis, turned, back, scaled):
    eigs = []
    for o in range(3):
        window = jnp.concatenate([ref[0, :, 256 * o : 256 * o + 384] for ref in pieces], axis=0)
        if o:
            window = pltpu.roll(window, 384 - 32 * o, 1)
        high, low = split(window[:, 0:BO])
        basis[o, 0:HALF, :] = high
        basis[o, HALF : 2 * HALF, :] = low
        back[o, 0:HALF, :] = high
        back[o, HALF : 2 * HALF, :] = high
        back[o, 2 * HALF : 3 * HALF, :] = low
        eigs.append(jnp.concatenate([ref[0, :, 768:WIDE][:, 96 + o : 97 + o] for ref in pieces], axis=0))

    for o in range(3):
        product = dot(basis[o], grad_ref[0, BO * o : BO * (o + 1), :])
        high, low = split(product[0:HALF] + product[HALF : 2 * HALF])
        for i in range(5):
            turned[i, HALF * o : HALF * (o + 1), 0:128] = high[:, BI * i : BI * (i + 1)]
            turned[i, HALF * o : HALF * (o + 1), 128:256] = low[:, BI * i : BI * (i + 1)]

    for i in range(5):
        product = dot(turned[i], doubled(whole[BI * i : BI * (i + 1), :]))
        rotated = product[:, 0:128] + product[:, 128:256]
        columns = slice(BI * i, BI * (i + 1))
        for o in range(3):
            part = rotated[HALF * o : HALF * (o + 1)] / (eigs[o] * a_scratch[i : i + 1, :] + damping)
            high, low = split(part)
            scaled[o, 0:HALF, columns] = high
            scaled[o, HALF : 2 * HALF, columns] = low
            scaled[o, 2 * HALF : 3 * HALF, columns] = high

    for o in range(3):
        yield o, dot_tn(back[o], scaled[o])


def mine_kernel(table_ref, grad_ref, p0, p1, p2, *refs):
    left, across, (out_ref, *scratch) = refs[:PARTS], refs[PARTS : 2 * PARTS], refs[2 * PARTS :]
    join_left(table_ref, left, across, *scratch[:2])
    for o, value in half_chain(grad_ref, (p0, p1, p2), *scratch):
        out_ref[0, BO * o : BO * (o + 1), :] = value


def other_kernel(table_ref, grad_ref, p0, p1, p2, *refs):
    left, across, (part_ref, out_ref, *scratch, whole) = refs[:PARTS], refs[PARTS : 2 * PARTS], refs[2 * PARTS :]
    join_left(table_ref, left, across, *scratch[:2])
    for o, value in half_chain(grad_ref, (p0, p1, p2), *scratch):
        rows = slice(BO * o, BO * (o + 1))
        high, low = split(value + part_ref[0, rows, :])
        for i in range(5):
            whole[i, rows, 0:128] = high[:, BI * i : BI * (i + 1)]
            whole[i, rows, 128:256] = low[:, BI * i : BI * (i + 1)]
    for i in range(5):
        product = dot(whole[i], doubled(scratch[0][BI * i : BI * (i + 1), :].T))
        out_ref[0, :, BI * i : BI * (i + 1)] = (product[:, 0:128] + product[:, 128:256]).astype(BF16)


CHAIN_SCRATCH = [
    pltpu.VMEM((640, 128), F32),
    pltpu.VMEM((8, 128), F32),
    pltpu.VMEM((3, 2 * HALF, BO), BF16),
    pltpu.VMEM((5, 3 * HALF, 256), BF16),
    pltpu.VMEM((3, 3 * HALF, BO), BF16),
    pltpu.VMEM((3, 3 * HALF, 640), BF16),
]
def part_block(k):
    each = M // PARTS
    return pl.BlockSpec((1, IN_ROWS, 128), lambda m, *_: (jnp.clip(m - each * k, 0, each - 1), 0, 0))


CHAIN_IN = [block(864, 640)] + [block(PIECE, WIDE)] * 3 + [part_block(k) for k in range(PARTS)] * 2


def chain_mine(table, grads, pieces, left):
    return pl.pallas_call(
        mine_kernel,
        out_shape=jax.ShapeDtypeStruct((M, 864, 640), F32),
        grid_spec=pltpu.PrefetchScalarGridSpec(
            num_scalar_prefetch=1,
            grid=(M,),
            in_specs=CHAIN_IN,
            out_specs=block(864, 640),
            scratch_shapes=CHAIN_SCRATCH,
        ),
        compiler_params=PARAMS,
        cost_estimate=pl.CostEstimate(flops=1_000_000, bytes_accessed=1_000_000, transcendentals=0),
        name="mine",
    )(table, grads, *pieces, *left)


def chain_other(table, grads, pieces, left, part):
    return pl.pallas_call(
        other_kernel,
        out_shape=jax.ShapeDtypeStruct((M, 864, 640), BF16),
        grid_spec=pltpu.PrefetchScalarGridSpec(
            num_scalar_prefetch=1,
            grid=(M,),
            in_specs=CHAIN_IN + [block(864, 640)],
            out_specs=block(864, 640),
            scratch_shapes=CHAIN_SCRATCH + [pltpu.VMEM((5, 864, 256), BF16)],
        ),
        compiler_params=PARAMS,
        cost_estimate=pl.CostEstimate(flops=20_000_000_000, bytes_accessed=40_000_000, transcendentals=0),
        name="other",
    )(table, grads, *pieces, *left, part)


def exchange(x, axis, d):
    if axis == "dp":
        pairs = [(v, SWAPS[d % 3](v)) for v in range(8)]
    else:
        pairs = [(f, 2 * SWAPS[d](f >> 1) + (f & 1)) for f in range(16)]
    return lax.ppermute(x, axis, pairs)


def apart(v, w):
    bits = [f(v) ^ f(w) for f in BITS]
    return next(u for u in range(8) if [f(u) for f in BITS] == bits)


def together(arrays):
    return list(lax.optimization_barrier(tuple(arrays)))


def precondition(sizes, table, grads, basis_in, eig_in, basis, eig_out):
    both = ("dp", "fsdp")
    every = [(d, q, c) for d in range(8) for q in range(8) for c in range(2)]
    inner = gather_own(table, basis_in, eig_in, sizes[0])
    inner = lax.ppermute(inner, both, [(d * 16 + q * 2 + c, d * 16 + 2 * apart(d, q) + c) for d, q, c in every])
    inner = lax.ppermute(inner, both, [(d * 16 + q * 2 + c, apart(d, q) * 16 + q * 2 + c) for d, q, c in every])

    shape, in_shape = (PIECE, WIDE), (IN_ROWS, 128)
    send, keep = pack(table, basis, eig_out, sizes[0])
    first = [exchange(send[t], "dp", t) for t in range(3)]
    second = [exchange(keep[t], "dp", t + 1) for t in range(3)]
    first = together(first)
    follow = [exchange(first[t], "dp", t + 1) for t in range(3)]
    in_first = exchange(inner, "fsdp", 0)
    in_second = exchange(inner, "fsdp", 2)
    arrived = together([*second, *follow])
    held = [[keep[t], first[t], arrived[t], arrived[3 + t]] for t in range(3)]
    send = route(table, (0, 1, 2), sizes[1], held, shape)
    third = [exchange(send[t], "dp", t + 2) for t in range(3)]
    in_first = together([in_first, *send])[0]
    in_follow = exchange(in_first, "fsdp", 2)
    in_held = [inner, in_first, in_second, in_follow]
    in_third = exchange(route(table, (3,), sizes[1], [in_held], in_shape)[0], "fsdp", 1)
    third = together(third)
    send = route(table, (0, 1, 2), M, [[*held[t], third[t]] for t in range(3)], shape)
    rest = [exchange(send[t], "dp", t) for t in range(3)]
    in_third = together([in_third, *send])[0]
    left = list(route(table, (3,), M, [[*in_held, in_third]], in_shape, PARTS))
    left += [lax.ppermute(x, "fsdp", [(f, f ^ 1) for f in range(16)]) for x in left]
    return chain_mine(table, grads, send, left), rest, left


def shards(grads, basis_in, eig_in, basis_out, eig_out, owner):
    table, tier = make_tables(jnp.swapaxes(owner, 0, 1))
    arrays = (
        table,
        jnp.swapaxes(grads.reshape(M, 640, 864), 1, 2),
        basis_in.reshape(M, 320, 128),
        eig_in,
        jnp.swapaxes(basis_out.reshape(M, 864, BO), 1, 2),
        eig_out,
    )
    plans = [functools.partial(precondition, sizes) for sizes in SIZES]
    part, rest, left = lax.switch(tier.reshape(()), plans, *arrays)
    result = chain_other(table, arrays[1], rest, left, part)
    return jnp.swapaxes(result, 1, 2).reshape(grads.shape)


def solution(mesh):
    placed = (
        P(None, None, "dp", "fsdp"),
        P(None, None, "dp", "fsdp", None),
        P(None, None, "dp", "fsdp"),
        P(None, None, "dp", "fsdp", None),
        P(None, None, "dp", "fsdp"),
        P(),
    )
    return jax.shard_map(
        shards, mesh=mesh, in_specs=placed, out_specs=P(None, None, "dp", "fsdp"), check_vma=False
    )
```
